512 devices in a mesh: blk: 32 (over z, x), tok: 16 (over y, core).
Axes of the slice: x: 4, y: 8, z: 8, core: 2. Of those that a mesh axis runs over, the one named last changes fastest.
Arguments:
- activations: bfloat16 [6144, 16384], P('tok', 'blk'), may hold values from -6 to 6
- weights: bfloat16 [6, 64, 2, 256, 256], P(None, 'blk', None, 'tok'), may hold values from -0.25 to 0.25
- matchings: int32 [6, 64], replicated, may hold values from 0 to 63, as said below
- cotangent: bfloat16 [6144, 16384], P('tok', 'blk'), may hold values from -6 to 6
Outputs:
- output: bfloat16 [6144, 16384], P('tok', 'blk')
- input_grad: bfloat16 [6144, 16384], P('tok', 'blk')
- weight_grad: float32 [6, 64, 2, 256, 256], P(None, 'blk', None, 'tok')
The draws below stay inside these ranges and needn't reach their ends.
Inputs may be any that keep to these rules, and one draw needn't show every extreme that they name: matchings[s] sends each block i either to itself or to i XOR 2^s, and the two blocks of each such pair make the same choice.
All inputs are finite; a program needn't handle non-finite values.
Results may differ from the reference program's by a relative error of at most 0.03.
Values may be sent and summed in bfloat16 or wider, within the bound.
No kernel may reach another device: no remote copies, remote signals or barrier semaphores. Data moves between devices by JAX's collectives and lax.ppermute only.
A program may use at most 64 MiB of HBM per device.

```python
import jax
import jax.numpy as jnp
from jax import lax

D = 16384
BS = 256
BLOCKS = 64
SECTIONS = 6
TOK_DEV = 384
TOKENS = 6144
N_TOK = 16


def draw_matchings(key, part):
    key = jax.random.fold_in(key, 7)
    ident = jnp.arange(BLOCKS, dtype=jnp.int32)
    rows = []
    for section in range(SECTIONS):
        span = 1 << section
        flips = jax.random.randint(jax.random.fold_in(key, section), (BLOCKS // 2,), 0, 2, dtype=jnp.int32)
        pair_index = ident // (2 * span) * span + ident % span
        flag = flips[pair_index]
        other = ident + span - 2 * span * (ident // span % 2)
        rows.append(jnp.where(flag == 1, other, ident))
    return jnp.stack(rows).astype(jnp.int32)


def level_of(stream_key, extent, cuts, low, high):
    factor_of, own = 1.0, jax.random.fold_in(stream_key, 6)
    for position, shards_of in cuts:
        draws = jnp.exp(jax.random.uniform(jax.random.fold_in(own, position), (shards_of,), jnp.float32, low / len(cuts), high / len(cuts)))
        factor_of = factor_of * jnp.repeat(draws, extent[position] // shards_of).reshape([-1 if axis == position else 1 for axis in range(len(extent))])
    return factor_of


def noise(own_key, shape, scale, reach, split=(), held_as=jnp.bfloat16):
    factor_of = level_of(own_key, shape, split, -0.22, 0.18) if split else 1.0
    array = jax.random.normal(own_key, shape, jnp.float32) * scale * factor_of
    return jnp.minimum(jnp.maximum(array, -reach), reach).astype(held_as)


def setup_inputs(seed: int = 0) -> dict:
    streams_of = jax.random.split(jax.random.key(seed), 5)
    return {
        "activations": noise(streams_of[0], (TOKENS, D), 1.0, 6.0, ((0, 16), (1, 32))),
        "weights": noise(streams_of[1], (SECTIONS, BLOCKS, 2, BS, BS), (2 * BS) ** -0.5, 0.25, ((1, 32), (3, 16))),
        "matchings": draw_matchings(jax.random.fold_in(streams_of[4], 71), 0),
        "cotangent": noise(streams_of[3], (TOKENS, D), 1.0, 6.0, ((0, 16), (1, 32))),
    }


def partner_of(value, section):
    rows, count, width = value.shape
    span = 1 << section
    shaped = value.reshape(rows, count // (2 * span), 2, span, width)
    return shaped[:, :, ::-1].reshape(rows, count, width)

def swapped_of(matchings, section):
    ident = jnp.arange(BLOCKS, dtype=jnp.int32)
    return (matchings[section] != ident)[None, :, None]

def group_pass(weights, matchings, acts, cotan):
    value = acts.reshape(TOK_DEV, BLOCKS, BS)
    saved = []
    final = None
    for section in range(SECTIONS):
        other = partner_of(value, section)
        flipped = swapped_of(matchings, section)
        first_in = jnp.where(flipped, other, value)
        second_in = jnp.where(flipped, value, other)
        saved.append((first_in, second_in))
        blocks = weights[section].astype(jnp.float32)
        mixed = jnp.einsum('tjk,jkl->tjl', first_in.astype(jnp.float32), blocks[:, 0])
        mixed = mixed + jnp.einsum('tjk,jkl->tjl', second_in.astype(jnp.float32), blocks[:, 1])
        if section < SECTIONS - 1:
            value = mixed.astype(jnp.bfloat16)
        else:
            final = mixed
    result = jax.nn.gelu(final).astype(jnp.bfloat16)
    back_fn = jax.vjp(jax.nn.gelu, final)[1]
    grad_now = back_fn(cotan.reshape(TOK_DEV, BLOCKS, BS).astype(jnp.float32))[0].astype(jnp.bfloat16)
    terms = [None] * SECTIONS
    for section in reversed(range(SECTIONS)):
        first_in, second_in = saved[section]
        grad_f = grad_now.astype(jnp.float32)
        terms[section] = jnp.stack([jnp.einsum('tjk,tjl->jkl', first_in.astype(jnp.float32), grad_f), jnp.einsum('tjk,tjl->jkl', second_in.astype(jnp.float32), grad_f)], axis=1)
        blocks = weights[section].astype(jnp.float32)
        grad_first = jnp.einsum('tjl,jkl->tjk', grad_f, blocks[:, 0])
        grad_second = jnp.einsum('tjl,jkl->tjk', grad_f, blocks[:, 1])
        flipped = swapped_of(matchings, section)
        kept = jnp.where(flipped, grad_second, grad_first)
        sent = jnp.where(flipped, grad_first, grad_second).astype(jnp.bfloat16)
        grad_now = (kept + partner_of(sent, section).astype(jnp.float32)).astype(jnp.bfloat16)
    rounded = lax.optimization_barrier(jnp.stack(terms).astype(jnp.bfloat16))
    return (result.reshape(TOK_DEV, D), grad_now.reshape(TOK_DEV, D), rounded)

def reference(activations, weights, matchings, cotangent):
    acts = activations.reshape(N_TOK, TOK_DEV, D)
    cotan = cotangent.reshape(N_TOK, TOK_DEV, D)

    def step_fn(total, pair):
        result, in_grad, rounded = group_pass(weights, matchings, pair[0], pair[1])
        return (total + rounded.astype(jnp.float32), (result, in_grad))
    start = jnp.zeros((SECTIONS, BLOCKS, 2, BS, BS), jnp.float32)
    total, outs = lax.scan(step_fn, start, (acts, cotan))
    return (outs[0].reshape(TOKENS, D), outs[1].reshape(TOKENS, D), total)
```

```python
import jax
import jax.numpy as jnp
from jax import lax
from jax.sharding import PartitionSpec as P


def partner(value, axis, bit):
    mask = 2**bit
    pairs = [(source, source ^ mask) for source in range(lax.axis_size(axis))]
    return lax.ppermute(value, axis, pairs)


def local_partner(value, section):
    count, rows, width = value.shape
    span = 1 << section
    shaped = value.reshape(count // (2 * span), 2, span, rows, width)
    return shaped[:, ::-1].reshape(count, rows, width)


def exchange(value, section, local_bits):
    if section < local_bits:
        return local_partner(value, section)
    return partner(value, "blk", section - local_bits)


def scatter_sum(terms, axis):
    count, per_dev, both, depth, width = terms.shape
    size = lax.axis_size(axis)
    parts = terms.reshape(count, per_dev, both, size, depth // size, width)
    parts = jnp.moveaxis(parts, 3, 0)
    parts = lax.all_to_all(parts, axis, 0, 0)
    return jnp.sum(parts.astype(jnp.float32), axis=0)


EARLY = 2


def body(activations, weights, matchings, cotangent):
    rows = activations.shape[0]
    sections, per_dev, _, _, width = weights.shape
    local_bits = per_dev.bit_length() - 1
    first_block = lax.axis_index("blk") * per_dev
    ident = first_block + jnp.arange(per_dev, dtype=jnp.int32)
    owned = lax.dynamic_slice_in_dim(matchings, first_block, per_dev, axis=1)
    flips = (owned != ident)[:, :, None, None]

    rest = lax.all_gather(weights[EARLY:], "tok", axis=3, tiled=True)
    full = [
        lax.all_gather(weights[s], "tok", axis=2, tiled=True) if s < EARLY else rest[s - EARLY]
        for s in range(sections)
    ]

    value = jnp.stack([activations[:, j * width : (j + 1) * width] for j in range(per_dev)])
    saved = []
    final = None
    for section in range(sections):
        other = exchange(value, section, local_bits)
        flipped = flips[section]
        first_in = jnp.where(flipped, other, value)
        second_in = jnp.where(flipped, value, other)
        saved.append((first_in, second_in))
        mixed = jnp.einsum("jtk,jkl->jtl", first_in, full[section][:, 0], preferred_element_type=jnp.float32)
        mixed = mixed + jnp.einsum(
            "jtk,jkl->jtl", second_in, full[section][:, 1], preferred_element_type=jnp.float32
        )
        if section < sections - 1:
            value = mixed.astype(jnp.bfloat16)
        else:
            final = mixed
    result = jax.nn.gelu(final).astype(jnp.bfloat16)
    back_fn = jax.vjp(jax.nn.gelu, final)[1]
    cotan = jnp.stack([cotangent[:, j * width : (j + 1) * width] for j in range(per_dev)])
    grad_now = back_fn(cotan.astype(jnp.float32))[0].astype(jnp.bfloat16)
    terms = [None] * sections
    late = None
    for section in reversed(range(sections)):
        first_in, second_in = saved[section]
        terms[section] = jnp.stack(
            [
                jnp.einsum("jtk,jtl->jkl", first_in, grad_now, preferred_element_type=jnp.float32),
                jnp.einsum("jtk,jtl->jkl", second_in, grad_now, preferred_element_type=jnp.float32),
            ],
            axis=1,
        ).astype(jnp.bfloat16)
        if section == EARLY:
            late = lax.psum_scatter(jnp.stack(terms[EARLY:]), "tok", scatter_dimension=3, tiled=True)
        grad_first = jnp.einsum(
            "jtl,jkl->jtk", grad_now, full[section][:, 0], preferred_element_type=jnp.float32
        )
        grad_second = jnp.einsum(
            "jtl,jkl->jtk", grad_now, full[section][:, 1], preferred_element_type=jnp.float32
        )
        flipped = flips[section]
        kept = jnp.where(flipped, grad_second, grad_first)
        sent = jnp.where(flipped, grad_first, grad_second).astype(jnp.bfloat16)
        grad_now = (kept + exchange(sent, section, local_bits).astype(jnp.float32)).astype(jnp.bfloat16)
    first = scatter_sum(jnp.stack(terms[:EARLY]), "tok")
    weight_grad = jnp.concatenate([first, late.astype(jnp.float32)])
    return (
        jnp.concatenate([result[j] for j in range(per_dev)], axis=1),
        jnp.concatenate([grad_now[j] for j in range(per_dev)], axis=1),
        weight_grad,
    )


def solution(mesh):
    placed = (P("tok", "blk"), P(None, "blk", None, "tok", None), P(), P("tok", "blk"))
    return jax.shard_map(
        body,
        mesh=mesh,
        in_specs=placed,
        out_specs=(P("tok", "blk"), P("tok", "blk"), P(None, "blk", None, "tok", None)),
        check_vma=False,
    )
```

```python
import jax
import jax.numpy as jnp
import numpy as np
from jax import lax
from jax.sharding import PartitionSpec as P


TRADED = {4: 3, 5: 4}
GATHERS = ((1, 2, 3), (4, 5))
SCATTERS = ((4, 5), (2, 3), (0, 1))


def flip(value, bit):
    mask = 1 << bit
    pairs = [(source, source ^ mask) for source in range(lax.axis_size("blk"))]
    return lax.ppermute(value, "blk", pairs)


def mine(bit):
    return (lax.axis_index("blk") >> bit) & 1


def trade(value, bit, axis=0):
    one = mine(bit) == 1
    low = lax.index_in_dim(value, 0, axis, keepdims=False)
    high = lax.index_in_dim(value, 1, axis, keepdims=False)
    keep = jnp.where(one, high, low)
    came = flip(jnp.where(one, low, high), bit)
    return jnp.stack([jnp.where(one, came, keep), jnp.where(one, keep, came)], axis)


def partner(value, section):
    if section == 0 or section in TRADED:
        return value[::-1]
    return flip(value, section - 1)


def owned_tables(sections):
    weight = np.zeros((5, sections, 1), np.int32)
    local = np.zeros((sections, 2), np.int32)
    place = {b + 1: b for b in range(5)}
    here = 0
    for section in range(sections):
        if section in TRADED:
            bit = TRADED[section]
            place[here] = bit
            del place[bit + 1]
            here = bit + 1
        for number, bit in place.items():
            weight[bit, section, 0] = 1 << number
        local[section] = np.arange(2) << here
    return weight, local


def swapped_blocks(matchings):
    sections, blocks = matchings.shape
    weight, local = owned_tables(sections)
    owned = sum((mine(bit) * weight[bit] for bit in range(5)), jnp.asarray(local))
    every = jnp.arange(blocks, dtype=jnp.int32)
    hit = (every == owned[:, :, None]) & (matchings != every)[:, None, :]
    return jnp.any(hit, axis=2)[:, :, None, None]


def scatter_sum(terms):
    count, per_dev, both, depth, width = terms.shape
    size = lax.axis_size("tok")
    core = lax.axis_index("tok") & 1
    parts = terms.reshape(count, per_dev, both, size // 2, 2, depth // size, width)
    parts = jnp.moveaxis(parts, (3, 4), (0, 1))
    even, odd = parts[:, 0], parts[:, 1]
    pairs = [(source, source ^ 1) for source in range(size)]
    came = lax.ppermute(jnp.where(core == 1, even, odd), "tok", pairs)
    kept = jnp.where(core == 1, odd, even)
    chip = (kept.astype(jnp.float32) + came.astype(jnp.float32)).astype(jnp.bfloat16)
    groups = [list(range(c, size, 2)) for c in range(2)]
    chip = lax.all_to_all(chip, "tok", 0, 0, axis_index_groups=groups)
    return jnp.sum(chip.astype(jnp.float32), axis=0)


def body(activations, weights, matchings, cotangent):
    rows = activations.shape[0]
    sections, per_dev, _, _, width = weights.shape

    flips = swapped_blocks(matchings)

    def split(array):
        return jnp.stack([array[:, j * width : (j + 1) * width] for j in range(per_dev)])

    def join(blocks):
        return jnp.concatenate([blocks[j] for j in range(per_dev)], axis=1)

    shards = {s: weights[s] for s in range(4)}
    moved = trade(weights[4:6], TRADED[4], axis=1)
    shards[4] = moved[0]
    shards[5] = trade(moved[1], TRADED[5])
    full = [None] * sections
    full[0] = lax.all_gather(shards[0], "tok", axis=2, tiled=True)
    for group in GATHERS:
        gathered = lax.all_gather(jnp.stack([shards[s] for s in group]), "tok", axis=3, tiled=True)
        for place, s in enumerate(group):
            full[s] = gathered[place]

    value = split(activations)
    saved = []
    for section in range(sections):
        if section in TRADED:
            value = trade(value, TRADED[section])
        flipped = flips[section]
        other = partner(value, section)
        first_in = jnp.where(flipped, other, value)
        second_in = jnp.where(flipped, value, other)
        saved.append((first_in, second_in, flipped))
        both = full[section]
        mixed = jnp.einsum("jtk,jkl->jtl", first_in, both[:, 0], preferred_element_type=jnp.float32)
        mixed = mixed + jnp.einsum(
            "jtk,jkl->jtl", second_in, both[:, 1], preferred_element_type=jnp.float32
        )
        if section < sections - 1:
            value = mixed.astype(jnp.bfloat16)
        if section == 0:
            cotan = split(lax.optimization_barrier((cotangent, value))[0])
            for at in sorted(TRADED):
                cotan = trade(cotan, TRADED[at])
    result = jax.nn.gelu(mixed).astype(jnp.bfloat16)
    back_fn = jax.vjp(jax.nn.gelu, mixed)[1]
    grad = back_fn(cotan.astype(jnp.float32))[0].astype(jnp.bfloat16)
    terms = [None] * sections
    totals = [None] * sections
    for section in reversed(range(sections)):
        first_in, second_in, flipped = saved[section]
        both = full[section]
        if section == 0:
            grad = lax.optimization_barrier((grad, totals[2]))[0]
        grad_first = jnp.einsum("jtl,jkl->jtk", grad, both[:, 0], preferred_element_type=jnp.float32)
        grad_second = jnp.einsum("jtl,jkl->jtk", grad, both[:, 1], preferred_element_type=jnp.float32)
        kept = jnp.where(flipped, grad_second, grad_first)
        sent = jnp.where(flipped, grad_first, grad_second).astype(jnp.bfloat16)
        term = jnp.stack(
            [
                jnp.einsum("jtk,jtl->jkl", part, grad, preferred_element_type=jnp.float32)
                for part in (first_in, second_in)
            ],
            axis=1,
        ).astype(jnp.bfloat16)
        terms[section] = term
        for group in SCATTERS:
            if section == min(group):
                summed = scatter_sum(jnp.stack([terms[s] for s in group]))
                for place, s in enumerate(group):
                    totals[s] = summed[place]
        if section == 2:
            sent = lax.optimization_barrier((sent, totals[4]))[0]
        grad = (kept + partner(sent, section).astype(jnp.float32)).astype(jnp.bfloat16)
        if section in TRADED:
            grad = trade(grad, TRADED[section])
    for at in sorted(TRADED, reverse=True):
        result = trade(result, TRADED[at])
    totals[5] = trade(totals[5], TRADED[5])
    moved = trade(jnp.stack(totals[4:6]), TRADED[4], axis=1)
    weight_grad = jnp.concatenate([jnp.stack(totals[:4]), moved])
    return join(result), join(grad), weight_grad


def solution(mesh):
    placed = (P("tok", "blk"), P(None, "blk", None, "tok", None), P(), P("tok", "blk"))
    return jax.shard_map(
        body,
        mesh=mesh,
        in_specs=placed,
        out_specs=(P("tok", "blk"), P("tok", "blk"), P(None, "blk", None, "tok", None)),
        check_vma=False,
    )
```

```python
import jax
import jax.numpy as jnp
import numpy as np
from jax import lax
from jax.sharding import PartitionSpec as P


SECTIONS = 6
GATHERS = ((0,), (1,), (2, 3), (4, 5))
SCATTERS = ((4, 5), (2, 3), (0, 1))


def flip(value, bit):
    mask = 1 << bit
    pairs = [(source, source ^ mask) for source in range(lax.axis_size("blk"))]
    return lax.ppermute(value, "blk", pairs)


def mine(bit):
    return (lax.axis_index("blk") >> bit) & 1


def after(value, other):
    probe = lax.squeeze(lax.slice(other, (0,) * other.ndim, (1,) * other.ndim), range(other.ndim))
    return jnp.where(probe != probe, jnp.zeros_like(value), value)


def dot(left, right):
    return jnp.einsum("...tk,...kl->...tl", left, right, preferred_element_type=jnp.float32)


def dot_back(left, right):
    return jnp.einsum("...tl,...kl->...tk", left, right, preferred_element_type=jnp.float32)


def dot_rows(left, right):
    return jnp.einsum("...tk,...tl->...kl", left, right, preferred_element_type=jnp.float32).astype(jnp.bfloat16)


def block_tables():
    weight = np.zeros((5, SECTIONS, 1), np.int32)
    for section in range(SECTIONS):
        place = {1: 0, 2: 1, 3: 2, 4: 3, 5: 4}
        if section >= 4:
            del place[4]
            place[0] = 3
        if section == 5:
            del place[5]
            place[4] = 4
        for number, bit in place.items():
            weight[bit, section, 0] = 1 << number
    local = np.array([1, 1, 1, 1, 16, 32], np.int32)[:, None]
    return weight, local


def choices(matchings):
    weight, local = block_tables()
    low, high = mine(3), mine(4)
    order = jnp.where(np.arange(SECTIONS)[:, None] < 4, low, high)
    rows = np.arange(2, dtype=np.int32)[None, :] ^ order
    owned = sum((mine(bit) * weight[bit] for bit in range(5)), rows * local)
    every = jnp.arange(matchings.shape[1], dtype=jnp.int32)
    hit = (every == owned[:, :, None]) & (matchings != every)[:, None, :]
    swapped = jnp.any(hit, axis=2)
    section = np.arange(SECTIONS)[:, None]
    turn = jnp.where(section == 4, rows ^ low, jnp.where(section == 5, rows ^ high, 0)) == 1
    return swapped ^ turn


def turned(value, yes, axis=0):
    low = lax.index_in_dim(value, 0, axis)
    high = lax.index_in_dim(value, 1, axis)
    return jnp.concatenate([jnp.where(yes, high, low), jnp.where(yes, low, high)], axis)


def core_half(terms, core):
    count, both, per_dev, size, depth, width = terms.shape
    parts = terms.reshape(count, both, per_dev, size // 2, 2, depth, width)
    half = jnp.where(core == 1, parts[:, :, :, :, 1], parts[:, :, :, :, 0])
    return jnp.moveaxis(half, 3, 0)


def scatter_sum(terms, waits):
    count, both, per_dev, depth, width = terms.shape
    size = lax.axis_size("tok")
    core = lax.axis_index("tok") & 1
    terms = terms.reshape(count, both, per_dev, size, depth // size, width)
    give = core_half(terms, 1 - core)
    if waits is not None:
        give = after(give, waits)
    came = lax.ppermute(give, "tok", [(source, source ^ 1) for source in range(size)])
    chip = (core_half(terms, core).astype(jnp.float32) + came.astype(jnp.float32)).astype(jnp.bfloat16)
    groups = [list(range(c, size, 2)) for c in range(2)]
    chip = lax.all_to_all(chip, "tok", 0, 0, axis_index_groups=groups)
    return jnp.sum(chip.astype(jnp.float32), axis=0)


def body(activations, weights, matchings, cotangent):
    width = weights.shape[4]
    bf16 = jnp.bfloat16
    low, high = mine(3) == 1, mine(4) == 1
    same = low == high
    chosen = choices(matchings)[:, None, :, None, None]

    def halves(array):
        return array[:, :width], array[:, width:]

    shards = jnp.swapaxes(weights, 1, 2)
    part = shards[4:6]
    keep = jnp.where(low, part[:, :, 1], part[:, :, 0])
    came = flip(jnp.where(low, part[:, :, 0], part[:, :, 1]), 3)
    row0, row1 = jnp.where(same, keep, came), jnp.where(same, came, keep)
    fourth = jnp.stack([row0[0], row1[0]], 1)
    fifth = jnp.stack([row0[1], flip(row1[1], 4)], 1)
    shards = [turned(shards[:4], low, 2), jnp.stack([fourth, fifth])]

    full = [None] * SECTIONS
    for group in GATHERS:
        source, base = (shards[0], 0) if group[0] < 4 else (shards[1], 4)
        begin, end = group[0] - base, group[-1] + 1 - base
        ordered = turned(source[begin:end], chosen[group[0] : group[-1] + 1], 1)
        gathered = lax.all_gather(ordered, "tok", axis=3, tiled=True)
        for place, section in enumerate(group):
            full[section] = gathered[place]

    left, right = halves(cotangent)
    came = flip(jnp.where(low, left, right), 3)
    keep = jnp.where(low, right, left)
    cotan0 = jnp.where(same, keep, came)
    cotan1 = flip(jnp.where(same, came, keep), 4)

    left, right = halves(activations)
    value = jnp.stack([jnp.where(low, right, left), jnp.where(low, left, right)])
    inputs = []
    for section in range(4):
        other = value[::-1] if section == 0 else flip(value, section - 1)
        inputs.append((value, other))
        own_w, other_w = full[section][0], full[section][1]
        if section < 3:
            value = (dot(value, own_w) + dot(other, other_w)).astype(bf16)
        else:
            send = (dot(value[1], own_w[1]) + dot(other[1], other_w[1])).astype(bf16)
            keep = (dot(value[0], own_w[0]) + dot(other[0], other_w[0])).astype(bf16)
    came = flip(send, 3)
    inputs.append((keep, came))
    own_w, other_w = full[4][0], full[4][1]
    send = (dot(keep, own_w[1]) + dot(came, other_w[1])).astype(bf16)
    keep = (dot(keep, own_w[0]) + dot(came, other_w[0])).astype(bf16)
    came = flip(send, 4)
    inputs.append((keep, came))
    own_w, other_w = full[5][0], full[5][1]

    results, grads = [], []
    for row, cotan in enumerate((cotan0, cotan1)):
        final = dot(keep, own_w[row]) + dot(came, other_w[row])
        results.append(jax.nn.gelu(final).astype(bf16))
        back_fn = jax.vjp(jax.nn.gelu, final)[1]
        grads.append(back_fn(cotan.astype(jnp.float32))[0].astype(bf16))

    terms = [None] * SECTIONS
    for section in (5, 4):
        own_w, other_w = full[section][0], full[section][1]
        sent = (dot_back(grads[0], other_w[0]) + dot_back(grads[1], other_w[1])).astype(bf16)
        back = flip(sent, section - 1)
        kept = (dot_back(grads[0], own_w[0]) + dot_back(grads[1], own_w[1])).astype(bf16)
        terms[section] = jnp.stack(
            [jnp.stack([dot_rows(part, grad) for grad in grads]) for part in inputs[section]]
        )
        grads = [kept, back]
    sums = [None] * SECTIONS
    waits = None
    for section in (3, 2, 1, 0):
        own_w, other_w = full[section][0], full[section][1]
        if section == 3:
            back = [flip(dot_back(grads[r], other_w[r]).astype(bf16), 2) for r in range(2)]
            kept = [dot_back(grads[r], own_w[r]) for r in range(2)]
            terms[section] = jnp.stack(
                [jnp.stack([dot_rows(part[r], grads[r]) for r in range(2)]) for part in inputs[section]]
            )
            grad = jnp.stack([(kept[r] + back[r].astype(jnp.float32)).astype(bf16) for r in range(2)])
        else:
            if section == 2:
                late = grad
            sent = dot_back(grad, other_w).astype(bf16)
            back = sent[::-1] if section == 0 else flip(sent, section - 1)
            terms[section] = jnp.stack([dot_rows(part, grad) for part in inputs[section]])
            grad = (dot_back(grad, own_w) + back.astype(jnp.float32)).astype(bf16)
        for group in SCATTERS:
            if section == min(group) or (section == 3 and group == (4, 5)):
                summed = scatter_sum(jnp.stack([terms[s] for s in group]), waits)
                waits = summed
                for place, s in enumerate(group):
                    sums[s] = summed[place]

    came = flip(after(results[1], late), 4)
    keep, send = jnp.where(same, results[0], came), jnp.where(same, came, results[0])
    came = flip(send, 3)
    result = jnp.concatenate([jnp.where(low, came, keep), jnp.where(low, keep, came)], axis=1)
    input_grad = jnp.concatenate([jnp.where(low, grad[1], grad[0]), jnp.where(low, grad[0], grad[1])], axis=1)

    first = turned(turned(jnp.stack(sums[:4]), chosen[:4], 1), low, 2)
    last = turned(jnp.stack(sums[4:]), chosen[4:], 1)
    row0 = last[:, :, 0]
    row1 = jnp.stack([last[0, :, 1], flip(last[1, :, 1], 4)])
    keep, send = jnp.where(same, row0, row1), jnp.where(same, row1, row0)
    came = flip(send, 3)
    last = jnp.stack([jnp.where(low, came, keep), jnp.where(low, keep, came)], 2)
    weight_grad = jnp.swapaxes(jnp.concatenate([first, last]), 1, 2)
    return result, input_grad, weight_grad


def solution(mesh):
    placed = (P("tok", "blk"), P(None, "blk", None, "tok", None), P(), P("tok", "blk"))
    return jax.shard_map(
        body,
        mesh=mesh,
        in_specs=placed,
        out_specs=(P("tok", "blk"), P("tok", "blk"), P(None, "blk", None, "tok", None)),
        check_vma=False,
    )
```

```python
import jax
import jax.numpy as jnp
import numpy as np
from jax import lax
from jax.sharding import PartitionSpec as P


SECTIONS = 6


def flip(value, bit):
    mask = 1 << bit
    pairs = [(source, source ^ mask) for source in range(lax.axis_size("blk"))]
    return lax.ppermute(value, "blk", pairs)


def mine(bit):
    return (lax.axis_index("blk") >> bit) & 1


def after(value, other):
    probe = lax.squeeze(lax.slice(other, (0,) * other.ndim, (1,) * other.ndim), range(other.ndim))
    return jnp.where(probe != probe, jnp.zeros_like(value), value)


def dot(left, right):
    return jnp.einsum("...tk,...kl->...tl", left, right, preferred_element_type=jnp.float32)


def dot_back(left, right):
    return jnp.einsum("...tl,...kl->...tk", left, right, preferred_element_type=jnp.float32)


def dot_rows(left, right):
    return jnp.einsum("...tk,...tl->...kl", left, right, preferred_element_type=jnp.float32).astype(jnp.bfloat16)


def pack(small, large):
    return jnp.concatenate([small.reshape(-1, small.shape[-1]), large])


def unpack(packed, like):
    rows = like.size // like.shape[-1]
    return packed[:rows].reshape(like.shape), packed[rows:]


def block_tables():
    weight = np.zeros((5, SECTIONS, 1), np.int32)
    for section in range(SECTIONS):
        place = {1: 0, 2: 1, 3: 2, 4: 3, 5: 4}
        if section >= 4:
            del place[4]
            place[0] = 3
        if section == 5:
            del place[5]
            place[4] = 4
        for number, bit in place.items():
            weight[bit, section, 0] = 1 << number
    local = np.array([1, 1, 1, 1, 16, 32], np.int32)[:, None]
    return weight, local


def choices(matchings):
    weight, local = block_tables()
    low, high = mine(3), mine(4)
    order = jnp.where(np.arange(SECTIONS)[:, None] < 4, low, high)
    rows = np.arange(2, dtype=np.int32)[None, :] ^ order
    owned = sum((mine(bit) * weight[bit] for bit in range(5)), rows * local)
    every = jnp.arange(matchings.shape[1], dtype=jnp.int32)
    hit = (every == owned[:, :, None]) & (matchings != every)[:, None, :]
    swapped = jnp.any(hit, axis=2)
    section = np.arange(SECTIONS)[:, None]
    turn = jnp.where(section == 4, rows ^ low, jnp.where(section == 5, rows ^ high, 0)) == 1
    return swapped ^ turn


def turned(value, yes, axis=0):
    low = lax.index_in_dim(value, 0, axis)
    high = lax.index_in_dim(value, 1, axis)
    return jnp.concatenate([jnp.where(yes, high, low), jnp.where(yes, low, high)], axis)


def core_half(terms, core):
    count, both, per_dev, size, depth, width = terms.shape
    parts = terms.reshape(count, both, per_dev, size // 2, 2, depth, width)
    half = jnp.where(core == 1, parts[:, :, :, :, 1], parts[:, :, :, :, 0])
    return jnp.moveaxis(half, 3, 0)


def chip_sum(terms, waits):
    count, both, per_dev, depth, width = terms.shape
    size = lax.axis_size("tok")
    core = lax.axis_index("tok") & 1
    terms = terms.reshape(count, both, per_dev, size, depth // size, width)
    give = core_half(terms, 1 - core)
    if waits is not None:
        give = after(give, waits)
    came = lax.ppermute(give, "tok", [(source, source ^ 1) for source in range(size)])
    return (core_half(terms, core).astype(jnp.float32) + came.astype(jnp.float32)).astype(jnp.bfloat16)


def all_sum(chip):
    size = lax.axis_size("tok")
    groups = [list(range(c, size, 2)) for c in range(2)]
    chip = lax.all_to_all(chip, "tok", 0, 0, axis_index_groups=groups)
    return jnp.sum(chip.astype(jnp.float32), axis=0)


def body(activations, weights, matchings, cotangent):
    width = weights.shape[4]
    bf16 = jnp.bfloat16
    low, high = mine(3) == 1, mine(4) == 1
    same = low == high
    chosen = choices(matchings)[:, None, :, None, None]

    def halves(array):
        return array[:, :width], array[:, width:]

    shards = jnp.swapaxes(weights, 1, 2)
    part = shards[4:6]
    left, right = halves(cotangent)
    keep = jnp.where(low, part[:, :, 1], part[:, :, 0])
    cot_keep = jnp.where(low, right, left)
    send = jnp.where(low, part[:, :, 0], part[:, :, 1])
    came, cot_came = unpack(flip(pack(send, jnp.where(low, left, right)), 3), send)
    row0, row1 = jnp.where(same, keep, came), jnp.where(same, came, keep)
    cotan0 = jnp.where(same, cot_keep, cot_came)
    cot_send = jnp.where(same, cot_came, cot_keep)
    fourth = jnp.stack([row0[0], row1[0]], 1)

    early = turned(turned(shards[:4], low, 2), chosen[:4], 1)
    full = list(lax.all_gather(early[:1], "tok", axis=3, tiled=True))
    full += list(lax.all_gather(early[1:], "tok", axis=3, tiled=True))

    left, right = halves(activations)
    value = jnp.stack([jnp.where(low, right, left), jnp.where(low, left, right)])
    other = value[::-1]
    inputs = [(value, other)]
    value = (dot(value, full[0][0]) + dot(other, full[0][1])).astype(bf16)

    came, cotan1 = unpack(flip(pack(after(row1[1], value), cot_send), 4), row1[1])
    fifth = jnp.stack([row0[1], came], 1)
    late = turned(jnp.stack([fourth, fifth]), chosen[4:], 1)
    full += list(lax.all_gather(late, "tok", axis=3, tiled=True))

    for section in range(1, 4):
        other = flip(value, section - 1)
        inputs.append((value, other))
        own_w, other_w = full[section][0], full[section][1]
        if section < 3:
            value = (dot(value, own_w) + dot(other, other_w)).astype(bf16)
        else:
            send = (dot(value[1], own_w[1]) + dot(other[1], other_w[1])).astype(bf16)
            keep = (dot(value[0], own_w[0]) + dot(other[0], other_w[0])).astype(bf16)
    came = flip(send, 3)
    inputs.append((keep, came))
    own_w, other_w = full[4][0], full[4][1]
    send = (dot(keep, own_w[1]) + dot(came, other_w[1])).astype(bf16)
    keep = (dot(keep, own_w[0]) + dot(came, other_w[0])).astype(bf16)
    came = flip(send, 4)
    inputs.append((keep, came))
    own_w, other_w = full[5][0], full[5][1]

    results, grads = [], []
    for row, cotan in enumerate((cotan0, cotan1)):
        final = dot(keep, own_w[row]) + dot(came, other_w[row])
        results.append(jax.nn.gelu(final).astype(bf16))
        back_fn = jax.vjp(jax.nn.gelu, final)[1]
        grads.append(back_fn(cotan.astype(jnp.float32))[0].astype(bf16))

    terms = [None] * SECTIONS
    for section in (5, 4):
        own_w, other_w = full[section][0], full[section][1]
        sent = (dot_back(grads[0], other_w[0]) + dot_back(grads[1], other_w[1])).astype(bf16)
        back = flip(sent, section - 1)
        kept = (dot_back(grads[0], own_w[0]) + dot_back(grads[1], own_w[1])).astype(bf16)
        terms[section] = jnp.stack(
            [jnp.stack([dot_rows(part, grad) for grad in grads]) for part in inputs[section]]
        )
        grads = [kept, back]
    chip = chip_sum(jnp.stack(terms[4:]), None)
    grad = after(jnp.stack(grads), chip)
    sums45 = all_sum(chip)
    for section in (3, 2, 1, 0):
        own_w, other_w = full[section][0], full[section][1]
        sent = dot_back(grad, other_w).astype(bf16)
        back = sent[::-1] if section == 0 else flip(sent, section - 1)
        terms[section] = jnp.stack([dot_rows(part, grad) for part in inputs[section]])
        grad = (dot_back(grad, own_w) + back.astype(jnp.float32)).astype(bf16)
        if section == 2:
            chip = chip_sum(jnp.stack(terms[2:4]), None)
            grad = after(after(grad, chip), sums45)
            sums23 = all_sum(chip)
        if section == 1:
            near_end = grad
    sums01 = all_sum(chip_sum(jnp.stack(terms[:2]), sums23))
    input_grad = jnp.concatenate([jnp.where(low, grad[1], grad[0]), jnp.where(low, grad[0], grad[1])], axis=1)

    first = turned(turned(jnp.concatenate([sums01, sums23]), chosen[:4], 1), low, 2)
    last = turned(sums45, chosen[4:], 1).astype(bf16)
    came, out_came = unpack(flip(pack(after(last[1, :, 1], near_end), results[1]), 4), last[1, :, 1])
    row0 = last[:, :, 0]
    row1 = jnp.stack([last[0, :, 1], came])
    keep, send = jnp.where(same, row0, row1), jnp.where(same, row1, row0)
    out_keep, out_send = jnp.where(same, results[0], out_came), jnp.where(same, out_came, results[0])
    came, out_came = unpack(flip(pack(send, out_send), 3), send)
    last = jnp.stack([jnp.where(low, came, keep), jnp.where(low, keep, came)], 2).astype(jnp.float32)
    result = jnp.concatenate([jnp.where(low, out_came, out_keep), jnp.where(low, out_keep, out_came)], axis=1)
    weight_grad = jnp.swapaxes(jnp.concatenate([first, last]), 1, 2)
    return result, input_grad, weight_grad


def solution(mesh):
    placed = (P("tok", "blk"), P(None, "blk", None, "tok", None), P(), P("tok", "blk"))
    return jax.shard_map(
        body,
        mesh=mesh,
        in_specs=placed,
        out_specs=(P("tok", "blk"), P("tok", "blk"), P(None, "blk", None, "tok", None)),
        check_vma=False,
    )
```

```python
import math

import jax
import jax.numpy as jnp
from jax import lax
from jax.experimental import pallas as pl
from jax.experimental.pallas import tpu as pltpu
from jax.sharding import PartitionSpec as P


SECTIONS = 6


def flip(value, bit):
    mask = 1 << bit
    pairs = [(source, source ^ mask) for source in range(lax.axis_size("blk"))]
    return lax.ppermute(value, "blk", pairs)


def after(value, other):
    start = (0,) * other.ndim
    probe = lax.slice(other, start, (1,) * (other.ndim - 1) + other.shape[-1:]).reshape(other.shape[-1])
    return jnp.where(probe != probe, jnp.zeros_like(value), value)


def dot(left, right):
    return jnp.einsum("...tk,...kl->...tl", left, right, preferred_element_type=jnp.float32)


def dot_back(left, right):
    return jnp.einsum("...tl,...kl->...tk", left, right, preferred_element_type=jnp.float32)


def dot_rows(left, right):
    return jnp.einsum("...tk,...tl->...kl", left, right, preferred_element_type=jnp.float32).astype(jnp.bfloat16)


def unpack(packed, shape):
    rows = math.prod(shape[:-1])
    return packed[:rows].reshape(shape), packed[rows:]


def bits():
    index = lax.axis_index("blk")
    return index, (index >> 3) & 1, (index >> 4) & 1


def choice(matchings, section, row):
    index, low, high = bits()
    if section < 4:
        block = (row ^ low) + 2 * index
        turn = 0
    elif section == 4:
        block = low + 2 * (index & 7) + 16 * (row ^ high) + 32 * high
        turn = row ^ high ^ low
    else:
        block = low + 2 * (index & 7) + 16 * high + 32 * (row ^ high)
        turn = row
    return (matchings[section, block] != block).astype(jnp.int32) ^ turn


def prepare(matchings, weights, cotangent, first, rest, keep, packed):
    _, low, _ = bits()
    width = weights.shape[-1]
    depth = weights.shape[-2]
    for section in range(4):
        for row in range(2):
            at = choice(matchings, section, row)
            out = first.at[0] if section == 0 else rest.at[section - 1]
            out[0, row] = weights[section, row ^ low, at]
            out[1, row] = weights[section, row ^ low, 1 - at]
    for place in range(2):
        for both in range(2):
            keep[place, both] = weights[4 + place, low, both]
            packed[pl.ds((2 * place + both) * depth, depth)] = weights[4 + place, 1 - low, both]
    packed[4 * depth :] = jnp.where(low == 1, cotangent[:, :width], cotangent[:, width:])


def between(matchings, keep, came, cotangent, fourth, fifth, packed, cotan):
    _, low, high = bits()
    width = keep.shape[-1]
    depth = keep.shape[-2]
    same = low == high

    def came_at(place, both):
        return came[pl.ds(pl.multiple_of((2 * place + both) * depth, depth), depth)]

    for row in range(2):
        at = choice(matchings, 4, row)
        own = same if row == 0 else jnp.logical_not(same)
        for slot, both in enumerate((at, 1 - at)):
            fourth[slot, row] = jnp.where(own, keep[0, both], came_at(0, both))
    for both in range(2):
        mine5, yours5 = keep[1, both], came_at(1, both)
        fifth[both] = jnp.where(same, mine5, yours5)
        packed[pl.ds(both * depth, depth)] = jnp.where(same, yours5, mine5)
    cot_keep = jnp.where(low == 1, cotangent[:, width:], cotangent[:, :width])
    cot_came = came[4 * depth :]
    cotan[...] = jnp.where(same, cot_keep, cot_came)
    packed[2 * depth :] = jnp.where(same, cot_came, cot_keep)


def gather_late(matchings, fourth, fifth, came, late):
    depth = fourth.shape[-2]
    late[0] = fourth[...]
    for row in range(2):
        at = choice(matchings, 5, row)
        for slot, both in enumerate((at, 1 - at)):
            if row == 0:
                late[1, slot, row] = fifth[both]
            else:
                late[1, slot, row] = came[pl.ds(pl.multiple_of(both * depth, depth), depth)]


def total(parts, place, slot, row):
    parts = [parts[chip, place, slot, row].astype(jnp.float32) for chip in range(parts.shape[0])]
    while len(parts) > 1:
        parts = [a + b for a, b in zip(parts[::2], parts[1::2])]
    return parts[0]


def unorder_late(matchings, parts, rows):
    for place in range(2):
        for row in range(2):
            at = choice(matchings, 4 + place, row)
            for slot, both in enumerate((at, 1 - at)):
                rows[row, place, both] = total(parts, 1 + place, slot, row).astype(rows.dtype)


def finish(matchings, parts_low, parts_high, keep, came, out):
    _, low, _ = bits()
    depth = out.shape[-2]
    for section in range(4):
        parts = parts_low if section < 3 else parts_high
        for row in range(2):
            at = choice(matchings, section, row)
            for slot, both in enumerate((at, 1 - at)):
                out[section, row ^ low, both] = total(parts, section % 3, slot, row)
    for place in range(2):
        for both in range(2):
            out[4 + place, low, both] = keep[place, both].astype(jnp.float32)
            given = came[pl.ds((2 * place + both) * depth, depth)]
            out[4 + place, 1 - low, both] = given.astype(jnp.float32)


def local(kernel, matchings, *arrays, outs):
    whole = pl.BlockSpec(memory_space=pltpu.VMEM)
    moved = sum(math.prod(x.shape) * x.dtype.itemsize for x in (*arrays, *outs))
    result = pl.pallas_call(
        kernel,
        out_shape=outs,
        in_specs=[pl.BlockSpec(memory_space=pltpu.SMEM)] + [whole] * len(arrays),
        out_specs=[whole] * len(outs),
        cost_estimate=pl.CostEstimate(flops=0, bytes_accessed=moved, transcendentals=0),
        compiler_params=pltpu.CompilerParams(vmem_limit_bytes=16 * 2**20),
    )(matchings, *arrays)
    return result[0] if len(outs) == 1 else result


def core_half(terms, core):
    count, both, per_dev, size, depth, width = terms.shape
    parts = terms.reshape(count, both, per_dev, size // 2, 2, depth, width)
    half = jnp.where(core == 1, parts[:, :, :, :, 1], parts[:, :, :, :, 0])
    return jnp.moveaxis(half, 3, 0)


def chip_sum(terms, waits):
    count, both, per_dev, depth, width = terms.shape
    size = lax.axis_size("tok")
    core = lax.axis_index("tok") & 1
    terms = terms.reshape(count, both, per_dev, size, depth // size, width)
    give = core_half(terms, 1 - core)
    if waits is not None:
        give = after(give, waits)
    came = lax.ppermute(give, "tok", [(source, source ^ 1) for source in range(size)])
    return (core_half(terms, core).astype(jnp.float32) + came.astype(jnp.float32)).astype(jnp.bfloat16)


def all_parts(chip):
    size = lax.axis_size("tok")
    groups = [list(range(c, size, 2)) for c in range(2)]
    return lax.all_to_all(chip, "tok", 0, 0, axis_index_groups=groups)


def body(activations, weights, matchings, cotangent):
    depth, width = weights.shape[3:]
    tokens = activations.shape[0]
    bf16 = jnp.bfloat16
    _, low, high = bits()
    low, same = low == 1, low == high

    def shape(*dims, dtype=bf16):
        return jax.ShapeDtypeStruct((*dims, width), dtype)

    first, rest, keep, packed = local(
        prepare,
        matchings,
        weights,
        cotangent,
        outs=[shape(1, 2, 2, depth), shape(3, 2, 2, depth), shape(2, 2, depth), shape(4 * depth + tokens)],
    )
    came = flip(packed, 3)
    full = list(lax.all_gather(first, "tok", axis=3, tiled=True))
    full += list(lax.all_gather(rest, "tok", axis=3, tiled=True))

    left, right = activations[:, :width], activations[:, width:]
    value = jnp.stack([jnp.where(low, right, left), jnp.where(low, left, right)])
    other = value[::-1]
    inputs = [(value, other)]
    value = (dot(value, full[0][0]) + dot(other, full[0][1])).astype(bf16)

    fourth, fifth, packed, cotan0 = local(
        between,
        matchings,
        keep,
        came,
        cotangent,
        outs=[shape(2, 2, depth), shape(2, depth), shape(2 * depth + tokens), shape(tokens)],
    )
    came = flip(packed, 4)
    cotan1 = came[2 * depth :]
    late = local(gather_late, matchings, fourth, fifth, came, outs=[shape(2, 2, 2, depth)])
    full += list(lax.all_gather(late, "tok", axis=3, tiled=True))

    for section in range(1, 4):
        other = flip(value, section - 1)
        inputs.append((value, other))
        own_w, other_w = full[section][0], full[section][1]
        if section < 3:
            value = (dot(value, own_w) + dot(other, other_w)).astype(bf16)
        else:
            send = (dot(value[1], own_w[1]) + dot(other[1], other_w[1])).astype(bf16)
            keep = (dot(value[0], own_w[0]) + dot(other[0], other_w[0])).astype(bf16)
    came = flip(send, 3)
    inputs.append((keep, came))
    own_w, other_w = full[4][0], full[4][1]
    send = (dot(keep, own_w[1]) + dot(came, other_w[1])).astype(bf16)
    keep = (dot(keep, own_w[0]) + dot(came, other_w[0])).astype(bf16)
    came = flip(send, 4)
    inputs.append((keep, came))
    own_w, other_w = full[5][0], full[5][1]

    results, grads = [], []
    for row, cotan in enumerate((cotan0, cotan1)):
        final = dot(keep, own_w[row]) + dot(came, other_w[row])
        results.append(jax.nn.gelu(final).astype(bf16))
        back_fn = jax.vjp(jax.nn.gelu, final)[1]
        grads.append(back_fn(cotan.astype(jnp.float32))[0].astype(bf16))

    terms = [None] * SECTIONS
    for section in (5, 4):
        own_w, other_w = full[section][0], full[section][1]
        sent = (dot_back(grads[0], other_w[0]) + dot_back(grads[1], other_w[1])).astype(bf16)
        back = flip(sent, section - 1)
        kept = (dot_back(grads[0], own_w[0]) + dot_back(grads[1], own_w[1])).astype(bf16)
        terms[section] = jnp.stack(
            [jnp.stack([dot_rows(part, grad) for grad in grads]) for part in inputs[section]]
        )
        grads = [kept, back]
    grad = jnp.stack(grads)
    for section in (3, 2, 1, 0):
        own_w, other_w = full[section][0], full[section][1]
        sent = dot_back(grad, other_w).astype(bf16)
        back = sent[::-1] if section == 0 else flip(sent, section - 1)
        terms[section] = jnp.stack([dot_rows(part, grad) for part in inputs[section]])
        if section == 3:
            chip = chip_sum(jnp.stack(terms[3:]), None)
            parts_high = all_parts(chip)
        grad = (dot_back(grad, own_w) + back.astype(jnp.float32)).astype(bf16)
        if section == 2:
            grad = after(grad, chip)
    chip = chip_sum(jnp.stack(terms[:3]), parts_high)
    parts_low = all_parts(chip)
    input_grad = jnp.concatenate([jnp.where(low, grad[1], grad[0]), jnp.where(low, grad[0], grad[1])], axis=1)

    rows = local(unorder_late, matchings, parts_high, outs=[shape(2, 2, 2, depth)])
    packed = jnp.concatenate([rows[1, 1].reshape(-1, width), after(results[1], chip)])
    came, out_came = unpack(flip(packed, 4), (2, depth, width))
    row0, row1 = rows[0], jnp.stack([rows[1, 0], came])
    keep, send = jnp.where(same, row0, row1), jnp.where(same, row1, row0)
    out_keep, out_send = jnp.where(same, results[0], out_came), jnp.where(same, out_came, results[0])
    packed = flip(jnp.concatenate([send.reshape(-1, width), out_send]), 3)
    out_came = packed[4 * depth :]
    result = jnp.concatenate([jnp.where(low, out_came, out_keep), jnp.where(low, out_keep, out_came)], axis=1)
    weight_grad = local(
        finish, matchings, parts_low, parts_high, keep, packed, outs=[shape(6, 2, 2, depth, dtype=jnp.float32)]
    )
    return result, input_grad, weight_grad


def solution(mesh):
    placed = (P("tok", "blk"), P(None, "blk", None, "tok", None), P(), P("tok", "blk"))
    return jax.shard_map(
        body,
        mesh=mesh,
        in_specs=placed,
        out_specs=(P("tok", "blk"), P("tok", "blk"), P(None, "blk", None, "tok", None)),
        check_vma=False,
    )
```

```python
import math

import jax
import jax.numpy as jnp
from jax import lax
from jax.experimental import pallas as pl
from jax.experimental.pallas import tpu as pltpu
from jax.sharding import PartitionSpec as P


SECTIONS = 6


def flip(value, bit):
    mask = 1 << bit
    pairs = [(source, source ^ mask) for source in range(lax.axis_size("blk"))]
    return lax.ppermute(value, "blk", pairs)


def after(value, other):
    start = (0,) * other.ndim
    probe = lax.slice(other, start, (1,) * (other.ndim - 1) + other.shape[-1:]).reshape(other.shape[-1])
    return jnp.where(probe != probe, jnp.zeros_like(value), value)


def dot(left, right):
    return jnp.einsum("...tk,...kl->...tl", left, right, preferred_element_type=jnp.float32)


def dot_back(left, right):
    return jnp.einsum("...tl,...kl->...tk", left, right, preferred_element_type=jnp.float32)


def dot_rows(left, right):
    return jnp.einsum("...tk,...tl->...kl", left, right, preferred_element_type=jnp.float32).astype(jnp.bfloat16)


def bits():
    index = lax.axis_index("blk")
    return index, (index >> 3) & 1, (index >> 4) & 1


def choice(matchings, section, row):
    index, low, high = bits()
    if section < 4:
        block = (row ^ low) + 2 * index
        turn = 0
    elif section == 4:
        block = low + 2 * (index & 7) + 16 * (row ^ high) + 32 * high
        turn = row ^ high ^ low
    else:
        block = low + 2 * (index & 7) + 16 * high + 32 * (row ^ high)
        turn = row
    return (matchings[section, block] != block).astype(jnp.int32) ^ turn


def order_early(matchings, weights, first, rest):
    _, low, _ = bits()
    for section in range(4):
        for row in range(2):
            at = choice(matchings, section, row)
            out = first.at[0] if section == 0 else rest.at[section - 1]
            out[0, row] = weights[section, row ^ low, at]
            out[1, row] = weights[section, row ^ low, 1 - at]


def pack_late(matchings, weights, cotangent, keep, packed):
    _, low, _ = bits()
    width = weights.shape[-1]
    depth = weights.shape[-2]
    for place in range(2):
        for both in range(2):
            keep[place, both] = weights[4 + place, low, both]
            packed[pl.ds((2 * place + both) * depth, depth)] = weights[4 + place, 1 - low, both]
    packed[4 * depth :] = jnp.where(low == 1, cotangent[:, :width], cotangent[:, width:])


def between(matchings, keep, came, cotangent, fourth, fifth, packed, cotan):
    _, low, high = bits()
    width = keep.shape[-1]
    depth = keep.shape[-2]
    same = low == high

    def came_at(place, both):
        return came[pl.ds(pl.multiple_of((2 * place + both) * depth, depth), depth)]

    for row in range(2):
        at = choice(matchings, 4, row)
        own = same if row == 0 else jnp.logical_not(same)
        for slot, both in enumerate((at, 1 - at)):
            fourth[slot, row] = jnp.where(own, keep[0, both], came_at(0, both))
    for both in range(2):
        mine5, yours5 = keep[1, both], came_at(1, both)
        fifth[both] = jnp.where(same, mine5, yours5)
        packed[pl.ds(both * depth, depth)] = jnp.where(same, yours5, mine5)
    cot_keep = jnp.where(low == 1, cotangent[:, width:], cotangent[:, :width])
    cot_came = came[4 * depth :]
    cotan[...] = jnp.where(same, cot_keep, cot_came)
    packed[2 * depth :] = jnp.where(same, cot_came, cot_keep)


def gather_late(matchings, fourth, fifth, came, late):
    depth = fourth.shape[-2]
    late[0] = fourth[...]
    for row in range(2):
        at = choice(matchings, 5, row)
        for slot, both in enumerate((at, 1 - at)):
            if row == 0:
                late[1, slot, row] = fifth[both]
            else:
                late[1, slot, row] = came[pl.ds(pl.multiple_of(both * depth, depth), depth)]


def total(parts, place, slot, row):
    parts = [parts[chip, place, slot, row].astype(jnp.float32) for chip in range(parts.shape[0])]
    while len(parts) > 1:
        parts = [a + b for a, b in zip(parts[::2], parts[1::2])]
    return parts[0]


def unorder_late(matchings, parts, rows):
    for place in range(2):
        for row in range(2):
            at = choice(matchings, 4 + place, row)
            for slot, both in enumerate((at, 1 - at)):
                rows[row, place, both] = total(parts, 1 + place, slot, row).astype(rows.dtype)


def finish(matchings, parts_low, parts_high, keep, came, out):
    _, low, _ = bits()
    depth = out.shape[-2]
    for section in range(4):
        parts = parts_low if section < 3 else parts_high
        for row in range(2):
            at = choice(matchings, section, row)
            for slot, both in enumerate((at, 1 - at)):
                out[section, row ^ low, both] = total(parts, section % 3, slot, row)
    for place in range(2):
        for both in range(2):
            out[4 + place, low, both] = keep[place, both].astype(jnp.float32)
            given = came[pl.ds((2 * place + both) * depth, depth)]
            out[4 + place, 1 - low, both] = given.astype(jnp.float32)


def local(kernel, matchings, *arrays, outs):
    whole = pl.BlockSpec(memory_space=pltpu.VMEM)
    moved = sum(math.prod(x.shape) * x.dtype.itemsize for x in (*arrays, *outs))
    result = pl.pallas_call(
        kernel,
        out_shape=outs,
        in_specs=[pl.BlockSpec(memory_space=pltpu.SMEM)] + [whole] * len(arrays),
        out_specs=[whole] * len(outs),
        cost_estimate=pl.CostEstimate(flops=0, bytes_accessed=moved, transcendentals=0),
        compiler_params=pltpu.CompilerParams(vmem_limit_bytes=16 * 2**20),
    )(matchings, *arrays)
    return result[0] if len(outs) == 1 else result


def core_half(terms, core):
    count, both, per_dev, size, depth, width = terms.shape
    parts = terms.reshape(count, both, per_dev, size // 2, 2, depth, width)
    half = jnp.where(core == 1, parts[:, :, :, :, 1], parts[:, :, :, :, 0])
    return jnp.moveaxis(half, 3, 0)


def chip_sum(terms):
    count, both, per_dev, depth, width = terms.shape
    size = lax.axis_size("tok")
    core = lax.axis_index("tok") & 1
    terms = terms.reshape(count, both, per_dev, size, depth // size, width)
    came = lax.ppermute(core_half(terms, 1 - core), "tok", [(source, source ^ 1) for source in range(size)])
    return (core_half(terms, core).astype(jnp.float32) + came.astype(jnp.float32)).astype(jnp.bfloat16)


def all_parts(chip):
    size = lax.axis_size("tok")
    groups = [list(range(c, size, 2)) for c in range(2)]
    return lax.all_to_all(chip, "tok", 0, 0, axis_index_groups=groups)


def body(activations, weights, matchings, cotangent):
    depth, width = weights.shape[3:]
    tokens = activations.shape[0]
    bf16 = jnp.bfloat16
    _, low, high = bits()
    low, same = low == 1, low == high

    def shape(*dims, dtype=bf16):
        return jax.ShapeDtypeStruct((*dims, width), dtype)

    first, rest = local(order_early, matchings, weights, outs=[shape(1, 2, 2, depth), shape(3, 2, 2, depth)])
    keep, packed = local(
        pack_late, matchings, weights, cotangent, outs=[shape(2, 2, depth), shape(4 * depth + tokens)]
    )
    came = flip(packed, 3)
    full = list(lax.all_gather(first, "tok", axis=3, tiled=True))
    full += list(lax.all_gather(rest, "tok", axis=3, tiled=True))

    left, right = activations[:, :width], activations[:, width:]
    value = jnp.stack([jnp.where(low, right, left), jnp.where(low, left, right)])
    other = value[::-1]
    inputs = [(value, other)]
    value = (dot(value, full[0][0]) + dot(other, full[0][1])).astype(bf16)

    fourth, fifth, packed, cotan0 = local(
        between,
        matchings,
        keep,
        came,
        cotangent,
        outs=[shape(2, 2, depth), shape(2, depth), shape(2 * depth + tokens), shape(tokens)],
    )
    came = flip(packed, 4)
    cotan1 = came[2 * depth :]
    late = local(gather_late, matchings, fourth, fifth, came, outs=[shape(2, 2, 2, depth)])
    full += list(lax.all_gather(late, "tok", axis=3, tiled=True))

    for section in range(1, 4):
        other = flip(value, section - 1)
        inputs.append((value, other))
        full[section] = after(full[section], value)
        own_w, other_w = full[section][0], full[section][1]
        if section < 3:
            value = (dot(value, own_w) + dot(other, other_w)).astype(bf16)
        else:
            send = (dot(value[1], own_w[1]) + dot(other[1], other_w[1])).astype(bf16)
            keep = (dot(value[0], own_w[0]) + dot(other[0], other_w[0])).astype(bf16)
    came = flip(send, 3)
    inputs.append((keep, came))
    full[4] = after(full[4], send)
    own_w, other_w = full[4][0], full[4][1]
    send = (dot(keep, own_w[1]) + dot(came, other_w[1])).astype(bf16)
    keep = (dot(keep, own_w[0]) + dot(came, other_w[0])).astype(bf16)
    came = flip(send, 4)
    inputs.append((keep, came))
    full[5] = after(full[5], send)
    own_w, other_w = full[5][0], full[5][1]

    results, grads = [], []
    for row, cotan in enumerate((cotan0, cotan1)):
        final = dot(keep, own_w[row]) + dot(came, other_w[row])
        results.append(jax.nn.gelu(final).astype(bf16))
        back_fn = jax.vjp(jax.nn.gelu, final)[1]
        grads.append(back_fn(cotan.astype(jnp.float32))[0].astype(bf16))

    terms = [None] * SECTIONS
    for section in (5, 4):
        own_w, other_w = full[section][0], full[section][1]
        sent = (dot_back(grads[0], other_w[0]) + dot_back(grads[1], other_w[1])).astype(bf16)
        back = flip(sent, section - 1)
        kept = (dot_back(grads[0], own_w[0]) + dot_back(grads[1], own_w[1])).astype(bf16)
        terms[section] = jnp.stack(
            [jnp.stack([dot_rows(part, grad) for grad in grads]) for part in inputs[section]]
        )
        grads = [kept, back]
    grad = jnp.stack(grads)
    for section in (3, 2, 1):
        own_w, other_w = full[section][0], full[section][1]
        sent = dot_back(grad, other_w).astype(bf16)
        back = flip(sent, section - 1)
        terms[section] = jnp.stack([dot_rows(part, grad) for part in inputs[section]])
        if section == 3:
            chip = chip_sum(jnp.stack(terms[3:]))
            parts_high = all_parts(chip)
        grad = (dot_back(grad, own_w) + back.astype(jnp.float32)).astype(bf16)
        if section == 2:
            grad = after(grad, chip)
    terms[0] = jnp.stack([dot_rows(part, grad) for part in inputs[0]])
    chip = after(chip_sum(jnp.stack(terms[:3])), parts_high)
    parts_low = all_parts(chip)

    out_came = flip(after(results[1], sent), 4)
    out_keep, out_send = jnp.where(same, results[0], out_came), jnp.where(same, out_came, results[0])
    out_came = flip(after(out_send, chip), 3)
    result = jnp.concatenate([jnp.where(low, out_came, out_keep), jnp.where(low, out_keep, out_came)], axis=1)

    rows = local(unorder_late, matchings, parts_high, outs=[shape(2, 2, 2, depth)])
    row0, row1 = rows[0], jnp.stack([rows[1, 0], flip(rows[1, 1], 4)])
    keep, send = jnp.where(same, row0, row1), jnp.where(same, row1, row0)
    came = flip(send, 3).reshape(4 * depth, width)
    weight_grad = local(
        finish, matchings, parts_low, parts_high, keep, came, outs=[shape(6, 2, 2, depth, dtype=jnp.float32)]
    )

    grad = after(grad, chip)
    own_w, other_w = full[0][0], full[0][1]
    first, second = [
        (dot_back(grad[r], own_w[r]) + dot_back(grad[1 - r], other_w[1 - r])).astype(bf16) for r in range(2)
    ]
    input_grad = jnp.concatenate([jnp.where(low, second, first), jnp.where(low, first, second)], axis=1)
    return result, input_grad, weight_grad


def solution(mesh):
    placed = (P("tok", "blk"), P(None, "blk", None, "tok", None), P(), P("tok", "blk"))
    return jax.shard_map(
        body,
        mesh=mesh,
        in_specs=placed,
        out_specs=(P("tok", "blk"), P("tok", "blk"), P(None, "blk", None, "tok", None)),
        check_vma=False,
    )
```

```python
import math

import jax
import jax.numpy as jnp
from jax import lax
from jax.experimental import pallas as pl
from jax.experimental.pallas import tpu as pltpu
from jax.sharding import PartitionSpec as P


SECTIONS = 6


def flip(value, bit):
    mask = 1 << bit
    pairs = [(source, source ^ mask) for source in range(lax.axis_size("blk"))]
    return lax.ppermute(value, "blk", pairs)


def after(value, other):
    start = (0,) * other.ndim
    probe = lax.slice(other, start, (1,) * (other.ndim - 1) + other.shape[-1:]).reshape(other.shape[-1])
    return jnp.where(probe != probe, jnp.zeros_like(value), value)


def dot(left, right):
    return jnp.einsum("...tk,...kl->...tl", left, right, preferred_element_type=jnp.float32)


def dot_back(left, right):
    return jnp.einsum("...tl,...kl->...tk", left, right, preferred_element_type=jnp.float32)


def dot_rows(left, right):
    return jnp.einsum("...tk,...tl->...kl", left, right, preferred_element_type=jnp.float32).astype(jnp.bfloat16)


def bits():
    index = lax.axis_index("blk")
    return index, (index >> 3) & 1, (index >> 4) & 1


def choice(matchings, section, row):
    index, low, high = bits()
    if section < 4:
        block = (row ^ low) + 2 * index
        turn = 0
    elif section == 4:
        block = low + 2 * (index & 7) + 16 * (row ^ high) + 32 * high
        turn = row ^ high ^ low
    else:
        block = low + 2 * (index & 7) + 16 * high + 32 * (row ^ high)
        turn = row
    return (matchings[section, block] != block).astype(jnp.int32) ^ turn


def order_early(matchings, weights, first, rest):
    _, low, _ = bits()
    for section in range(4):
        for row in range(2):
            at = choice(matchings, section, row)
            out = first.at[0] if section == 0 else rest.at[section - 1]
            out[row, 0] = weights[section, row ^ low, at]
            out[row, 1] = weights[section, row ^ low, 1 - at]


def pack_late(matchings, weights, cotangent, keep, packed):
    _, low, _ = bits()
    width = weights.shape[-1]
    depth = weights.shape[-2]
    for place in range(2):
        for both in range(2):
            keep[place, both] = weights[4 + place, low, both]
            packed[pl.ds((2 * place + both) * depth, depth)] = weights[4 + place, 1 - low, both]
    packed[4 * depth :] = jnp.where(low == 1, cotangent[:, :width], cotangent[:, width:])


def between(matchings, keep, came, cotangent, fourth, fifth, packed, cotan):
    _, low, high = bits()
    width = keep.shape[-1]
    depth = keep.shape[-2]
    same = low == high

    def came_at(place, both):
        return came[pl.ds(pl.multiple_of((2 * place + both) * depth, depth), depth)]

    for row in range(2):
        at = choice(matchings, 4, row)
        own = same if row == 0 else jnp.logical_not(same)
        for slot, both in enumerate((at, 1 - at)):
            fourth[row, slot] = jnp.where(own, keep[0, both], came_at(0, both))
    for both in range(2):
        mine5, yours5 = keep[1, both], came_at(1, both)
        fifth[both] = jnp.where(same, mine5, yours5)
        packed[pl.ds(both * depth, depth)] = jnp.where(same, yours5, mine5)
    cot_keep = jnp.where(low == 1, cotangent[:, width:], cotangent[:, :width])
    cot_came = came[4 * depth :]
    cotan[...] = jnp.where(same, cot_keep, cot_came)
    packed[2 * depth :] = jnp.where(same, cot_came, cot_keep)


def gather_late(matchings, fourth, fifth, came, late):
    depth = fourth.shape[-2]
    late[0] = fourth[...]
    for row in range(2):
        at = choice(matchings, 5, row)
        for slot, both in enumerate((at, 1 - at)):
            if row == 0:
                late[1, row, slot] = fifth[both]
            else:
                late[1, row, slot] = came[pl.ds(pl.multiple_of(both * depth, depth), depth)]


def total(parts, place, slot, row):
    parts = [parts[chip, place, slot, row].astype(jnp.float32) for chip in range(parts.shape[0])]
    while len(parts) > 1:
        parts = [a + b for a, b in zip(parts[::2], parts[1::2])]
    return parts[0]


def unorder_late(matchings, parts, rows):
    for place in range(2):
        for row in range(2):
            at = choice(matchings, 4 + place, row)
            for slot, both in enumerate((at, 1 - at)):
                rows[row, place, both] = total(parts, 1 + place, slot, row).astype(rows.dtype)


def finish(matchings, parts_low, parts_high, keep, came, out):
    _, low, _ = bits()
    depth = out.shape[-2]
    for section in range(4):
        parts = parts_low if section < 3 else parts_high
        for row in range(2):
            at = choice(matchings, section, row)
            for slot, both in enumerate((at, 1 - at)):
                out[section, row ^ low, both] = total(parts, section % 3, slot, row)
    for place in range(2):
        for both in range(2):
            out[4 + place, low, both] = keep[place, both].astype(jnp.float32)
            given = came[pl.ds((2 * place + both) * depth, depth)]
            out[4 + place, 1 - low, both] = given.astype(jnp.float32)


def local(kernel, matchings, *arrays, outs):
    whole = pl.BlockSpec(memory_space=pltpu.VMEM)
    moved = sum(math.prod(x.shape) * x.dtype.itemsize for x in (*arrays, *outs))
    result = pl.pallas_call(
        kernel,
        out_shape=outs,
        in_specs=[pl.BlockSpec(memory_space=pltpu.SMEM)] + [whole] * len(arrays),
        out_specs=[whole] * len(outs),
        cost_estimate=pl.CostEstimate(flops=0, bytes_accessed=moved, transcendentals=0),
        compiler_params=pltpu.CompilerParams(vmem_limit_bytes=16 * 2**20),
    )(matchings, *arrays)
    return result[0] if len(outs) == 1 else result


def row_terms(parts, grads):
    return jnp.stack([jnp.stack([dot_rows(part[r], grads[r]) for r in range(2)]) for part in parts])


def core_half(terms, core):
    count, both, per_dev, size, depth, width = terms.shape
    parts = terms.reshape(count, both, per_dev, size // 2, 2, depth, width)
    half = jnp.where(core == 1, parts[:, :, :, :, 1], parts[:, :, :, :, 0])
    return jnp.moveaxis(half, 3, 0)


def chip_sum(terms):
    count, both, per_dev, depth, width = terms.shape
    size = lax.axis_size("tok")
    core = lax.axis_index("tok") & 1
    terms = terms.reshape(count, both, per_dev, size, depth // size, width)
    came = lax.ppermute(core_half(terms, 1 - core), "tok", [(source, source ^ 1) for source in range(size)])
    return (core_half(terms, core).astype(jnp.float32) + came.astype(jnp.float32)).astype(jnp.bfloat16)


def all_parts(chip):
    size = lax.axis_size("tok")
    groups = [list(range(c, size, 2)) for c in range(2)]
    return lax.all_to_all(chip, "tok", 0, 0, axis_index_groups=groups)


def body(activations, weights, matchings, cotangent):
    depth, width = weights.shape[3:]
    tokens = activations.shape[0]
    bf16 = jnp.bfloat16
    _, low, high = bits()
    low, same = low == 1, low == high

    def shape(*dims, dtype=bf16):
        return jax.ShapeDtypeStruct((*dims, width), dtype)

    first, rest = local(order_early, matchings, weights, outs=[shape(1, 2, 2, depth), shape(3, 2, 2, depth)])
    keep, packed = local(
        pack_late, matchings, weights, cotangent, outs=[shape(2, 2, depth), shape(4 * depth + tokens)]
    )
    came = flip(packed, 3)
    full = list(lax.all_gather(first, "tok", axis=3, tiled=True))
    full += list(lax.all_gather(rest, "tok", axis=3, tiled=True))

    left, right = activations[:, :width], activations[:, width:]
    rows = [jnp.where(low, right, left), jnp.where(low, left, right)]
    inputs = [(rows, rows[::-1])]
    rows = [(dot(rows[r], full[0][r, 0]) + dot(rows[1 - r], full[0][r, 1])).astype(bf16) for r in range(2)]

    fourth, fifth, packed, cotan0 = local(
        between,
        matchings,
        keep,
        came,
        cotangent,
        outs=[shape(2, 2, depth), shape(2, depth), shape(2 * depth + tokens), shape(tokens)],
    )
    came = flip(packed, 4)
    cotan1 = came[2 * depth :]
    late = local(gather_late, matchings, fourth, fifth, came, outs=[shape(2, 2, 2, depth)])
    full += list(lax.all_gather(late, "tok", axis=3, tiled=True))

    for section in range(1, 4):
        second = flip(rows[1], section - 1)
        others = [flip(rows[0], section - 1), second]
        inputs.append((rows, others))
        second_w = after(full[section][1], rows[0])
        second = (dot(rows[1], second_w[0]) + dot(others[1], second_w[1])).astype(bf16)
        first_w = after(full[section][0], second)
        first = (dot(rows[0], first_w[0]) + dot(others[0], first_w[1])).astype(bf16)
        full[section] = [first_w, second_w]
        rows = [first, second]
    keep, send = rows
    came = flip(send, 3)
    inputs.append((keep, came))
    full[4] = after(full[4], send)
    send = (dot(keep, full[4][1, 0]) + dot(came, full[4][1, 1])).astype(bf16)
    keep = (dot(keep, full[4][0, 0]) + dot(came, full[4][0, 1])).astype(bf16)
    came = flip(send, 4)
    inputs.append((keep, came))
    full[5] = after(full[5], send)

    results, grads = [], []
    for row, cotan in enumerate((cotan0, cotan1)):
        final = dot(keep, full[5][row, 0]) + dot(came, full[5][row, 1])
        results.append(jax.nn.gelu(final).astype(bf16))
        back_fn = jax.vjp(jax.nn.gelu, final)[1]
        grads.append(back_fn(cotan.astype(jnp.float32))[0].astype(bf16))

    terms = [None] * SECTIONS
    for section in (5, 4):
        both = full[section]
        sent = (dot_back(grads[0], both[0, 1]) + dot_back(grads[1], both[1, 1])).astype(bf16)
        back = flip(sent, section - 1)
        kept = (dot_back(grads[0], both[0, 0]) + dot_back(grads[1], both[1, 0])).astype(bf16)
        terms[section] = jnp.stack(
            [jnp.stack([dot_rows(part, grad) for grad in grads]) for part in inputs[section]]
        )
        grads = [kept, back]
    before = sent
    for section in (3, 2, 1):
        both = full[section]
        sent = [dot_back(grads[r], both[r][1]).astype(bf16) for r in range(2)]
        sent[0] = after(sent[0], before)
        back = [flip(part, section - 1) for part in sent]
        terms[section] = row_terms(inputs[section], grads)
        if section == 3:
            chip = chip_sum(jnp.stack(terms[3:]))
            parts_high = all_parts(chip)
        grads = [
            (dot_back(grads[r], both[r][0]) + back[r].astype(jnp.float32)).astype(bf16) for r in range(2)
        ]
        before = sent[1]
        if section == 2:
            grads[0] = after(grads[0], chip)
    grads = [after(grads[r], sent[1 - r]) for r in range(2)]
    terms[0] = row_terms(inputs[0], grads)
    chip = after(chip_sum(jnp.stack(terms[:3])), parts_high)
    parts_low = all_parts(chip)

    out_came = flip(after(results[1], sent[1]), 4)
    out_keep, out_send = jnp.where(same, results[0], out_came), jnp.where(same, out_came, results[0])
    out_came = flip(after(out_send, chip), 3)
    result = jnp.concatenate([jnp.where(low, out_came, out_keep), jnp.where(low, out_keep, out_came)], axis=1)

    rows = local(unorder_late, matchings, parts_high, outs=[shape(2, 2, 2, depth)])
    row0, row1 = rows[0], jnp.stack([rows[1, 0], flip(rows[1, 1], 4)])
    keep, send = jnp.where(same, row0, row1), jnp.where(same, row1, row0)
    came = flip(send, 3).reshape(4 * depth, width)
    weight_grad = local(
        finish, matchings, parts_low, parts_high, keep, came, outs=[shape(6, 2, 2, depth, dtype=jnp.float32)]
    )

    grads = [after(grad, chip) for grad in grads]
    first, second = [
        (dot_back(grads[r], full[0][r, 0]) + dot_back(grads[1 - r], full[0][1 - r, 1])).astype(bf16)
        for r in range(2)
    ]
    input_grad = jnp.concatenate([jnp.where(low, second, first), jnp.where(low, first, second)], axis=1)
    return result, input_grad, weight_grad


def solution(mesh):
    placed = (P("tok", "blk"), P(None, "blk", None, "tok", None), P(), P("tok", "blk"))
    return jax.shard_map(
        body,
        mesh=mesh,
        in_specs=placed,
        out_specs=(P("tok", "blk"), P("tok", "blk"), P(None, "blk", None, "tok", None)),
        check_vma=False,
    )
```

```python
import math

import jax
import jax.numpy as jnp
from jax import lax
from jax.experimental import pallas as pl
from jax.experimental.pallas import tpu as pltpu
from jax.sharding import PartitionSpec as P


SECTIONS = 6


def flip(value, bit):
    mask = 1 << bit
    pairs = [(source, source ^ mask) for source in range(lax.axis_size("blk"))]
    return lax.ppermute(value, "blk", pairs)


def after(value, other):
    start = (0,) * other.ndim
    probe = lax.slice(other, start, (1,) * (other.ndim - 1) + other.shape[-1:]).reshape(other.shape[-1])
    return jnp.where(probe != probe, jnp.zeros_like(value), value)


def dot(left, right):
    return jnp.einsum("...tk,...kl->...tl", left, right, preferred_element_type=jnp.float32)


def dot_back(left, right):
    return jnp.einsum("...tl,...kl->...tk", left, right, preferred_element_type=jnp.float32)


def dot_rows(left, right):
    return jnp.einsum("...tk,...tl->...kl", left, right, preferred_element_type=jnp.float32).astype(jnp.bfloat16)


def bits():
    index = lax.axis_index("blk")
    return index, (index >> 3) & 1, (index >> 4) & 1


def choice(matchings, section, row):
    index, low, high = bits()
    if section < 4:
        block = (row ^ low) + 2 * index
        turn = 0
    elif section == 4:
        block = low + 2 * (index & 7) + 16 * (row ^ high) + 32 * high
        turn = row ^ high ^ low
    else:
        block = low + 2 * (index & 7) + 16 * high + 32 * (row ^ high)
        turn = row
    return (matchings[section, block] != block).astype(jnp.int32) ^ turn


def order_early(matchings, weights, first, rest):
    _, low, _ = bits()
    for section in range(4):
        for row in range(2):
            at = choice(matchings, section, row)
            out = first.at[0] if section == 0 else rest.at[section - 1]
            out[0, row] = weights[section, row ^ low, at]
            out[1, row] = weights[section, row ^ low, 1 - at]


def pack_late(matchings, weights, cotangent, keep, packed):
    _, low, _ = bits()
    width = weights.shape[-1]
    depth = weights.shape[-2]
    for place in range(2):
        for both in range(2):
            keep[place, both] = weights[4 + place, low, both]
            packed[pl.ds((2 * place + both) * depth, depth)] = weights[4 + place, 1 - low, both]
    packed[4 * depth :] = jnp.where(low == 1, cotangent[:, :width], cotangent[:, width:])


def between(matchings, keep, came, cotangent, fourth, fifth, packed, cotan):
    _, low, high = bits()
    width = keep.shape[-1]
    depth = keep.shape[-2]
    same = low == high

    def came_at(place, both):
        return came[pl.ds(pl.multiple_of((2 * place + both) * depth, depth), depth)]

    for row in range(2):
        at = choice(matchings, 4, row)
        own = same if row == 0 else jnp.logical_not(same)
        for slot, both in enumerate((at, 1 - at)):
            fourth[slot, row] = jnp.where(own, keep[0, both], came_at(0, both))
    for both in range(2):
        mine5, yours5 = keep[1, both], came_at(1, both)
        fifth[both] = jnp.where(same, mine5, yours5)
        packed[pl.ds(both * depth, depth)] = jnp.where(same, yours5, mine5)
    cot_keep = jnp.where(low == 1, cotangent[:, width:], cotangent[:, :width])
    cot_came = came[4 * depth :]
    cotan[...] = jnp.where(same, cot_keep, cot_came)
    packed[2 * depth :] = jnp.where(same, cot_came, cot_keep)


def gather_late(matchings, fourth, fifth, came, late):
    depth = fourth.shape[-2]
    late[0] = fourth[...]
    for row in range(2):
        at = choice(matchings, 5, row)
        for slot, both in enumerate((at, 1 - at)):
            if row == 0:
                late[1, slot, row] = fifth[both]
            else:
                late[1, slot, row] = came[pl.ds(pl.multiple_of(both * depth, depth), depth)]


def total(parts, place, slot, row):
    parts = [parts[chip, place, slot, row].astype(jnp.float32) for chip in range(parts.shape[0])]
    while len(parts) > 1:
        parts = [a + b for a, b in zip(parts[::2], parts[1::2])]
    return parts[0]


def unorder_late(matchings, parts, rows):
    for place in range(2):
        for row in range(2):
            at = choice(matchings, 4 + place, row)
            for slot, both in enumerate((at, 1 - at)):
                rows[row, place, both] = total(parts, 1 + place, slot, row).astype(rows.dtype)


def finish(matchings, parts_low, parts_high, keep, came, out):
    _, low, _ = bits()
    depth = out.shape[-2]
    for section in range(4):
        parts = parts_low if section < 3 else parts_high
        for row in range(2):
            at = choice(matchings, section, row)
            for slot, both in enumerate((at, 1 - at)):
                out[section, row ^ low, both] = total(parts, section % 3, slot, row)
    for place in range(2):
        for both in range(2):
            out[4 + place, low, both] = keep[place, both].astype(jnp.float32)
            given = came[pl.ds((2 * place + both) * depth, depth)]
            out[4 + place, 1 - low, both] = given.astype(jnp.float32)


def local(kernel, matchings, *arrays, outs):
    whole = pl.BlockSpec(memory_space=pltpu.VMEM)
    moved = sum(math.prod(x.shape) * x.dtype.itemsize for x in (*arrays, *outs))
    result = pl.pallas_call(
        kernel,
        out_shape=outs,
        in_specs=[pl.BlockSpec(memory_space=pltpu.SMEM)] + [whole] * len(arrays),
        out_specs=[whole] * len(outs),
        cost_estimate=pl.CostEstimate(flops=0, bytes_accessed=moved, transcendentals=0),
        compiler_params=pltpu.CompilerParams(vmem_limit_bytes=16 * 2**20),
    )(matchings, *arrays)
    return result[0] if len(outs) == 1 else result


def row_terms(parts, grads):
    return jnp.stack([jnp.stack([dot_rows(part[r], grads[r]) for r in range(2)]) for part in parts])


def spread(shards):
    size = lax.axis_size("tok")
    every = lax.all_to_all(jnp.broadcast_to(shards, (size, *shards.shape)), "tok", 0, 0)
    every = jnp.moveaxis(every, 0, 3)
    return list(every.reshape(*shards.shape[:3], size * shards.shape[3], shards.shape[4]))


def core_half(terms, core):
    count, both, per_dev, size, depth, width = terms.shape
    parts = terms.reshape(count, both, per_dev, size // 2, 2, depth, width)
    half = jnp.where(core == 1, parts[:, :, :, :, 1], parts[:, :, :, :, 0])
    return jnp.moveaxis(half, 3, 0)


def chip_sum(terms):
    count, both, per_dev, depth, width = terms.shape
    size = lax.axis_size("tok")
    core = lax.axis_index("tok") & 1
    terms = terms.reshape(count, both, per_dev, size, depth // size, width)
    came = lax.ppermute(core_half(terms, 1 - core), "tok", [(source, source ^ 1) for source in range(size)])
    return (core_half(terms, core).astype(jnp.float32) + came.astype(jnp.float32)).astype(jnp.bfloat16)


def all_parts(chip):
    size = lax.axis_size("tok")
    groups = [list(range(c, size, 2)) for c in range(2)]
    return lax.all_to_all(chip, "tok", 0, 0, axis_index_groups=groups)


def body(activations, weights, matchings, cotangent):
    depth, width = weights.shape[3:]
    tokens = activations.shape[0]
    bf16 = jnp.bfloat16
    _, low, high = bits()
    low, same = low == 1, low == high

    def shape(*dims, dtype=bf16):
        return jax.ShapeDtypeStruct((*dims, width), dtype)

    first, rest = local(order_early, matchings, weights, outs=[shape(1, 2, 2, depth), shape(3, 2, 2, depth)])
    keep, packed = local(
        pack_late, matchings, weights, cotangent, outs=[shape(2, 2, depth), shape(4 * depth + tokens)]
    )
    came = flip(packed, 3)
    full = list(lax.all_gather(first, "tok", axis=3, tiled=True))
    full += list(lax.all_gather(rest, "tok", axis=3, tiled=True))

    left, right = activations[:, :width], activations[:, width:]
    value = jnp.stack([jnp.where(low, right, left), jnp.where(low, left, right)])
    other = value[::-1]
    inputs = [(value, other)]
    value = (dot(value, full[0][0]) + dot(other, full[0][1])).astype(bf16)

    fourth, fifth, packed, cotan0 = local(
        between,
        matchings,
        keep,
        came,
        cotangent,
        outs=[shape(2, 2, depth), shape(2, depth), shape(2 * depth + tokens), shape(tokens)],
    )
    late = flip(packed, 4)
    cotan1 = late[2 * depth :]

    other = flip(value, 0)
    rows, others = [value[0], value[1]], [other[0], other[1]]
    for section in range(1, 4):
        if section > 1:
            second = flip(rows[1], section - 1)
            others = [flip(rows[0], section - 1), second]
        inputs.append((rows, others))
        weight = after(full[section], rows[0])
        first, second = [
            (dot(rows[r], weight[0, r]) + dot(others[r], weight[1, r])).astype(bf16) for r in range(2)
        ]
        full[section] = weight
        if section == 1:
            late = after(late, second)
            late = local(gather_late, matchings, fourth, fifth, late, outs=[shape(2, 2, 2, depth)])
            full += spread(late)
        rows = [first, second]
    keep, send = rows
    came = flip(send, 3)
    inputs.append((keep, came))
    full[4] = after(full[4], send)
    own_w, other_w = full[4][0], full[4][1]
    send = (dot(keep, own_w[1]) + dot(came, other_w[1])).astype(bf16)
    keep = (dot(keep, own_w[0]) + dot(came, other_w[0])).astype(bf16)
    came = flip(send, 4)
    inputs.append((keep, came))
    full[5] = after(full[5], send)
    own_w, other_w = full[5][0], full[5][1]

    results, grads = [], []
    for row, cotan in enumerate((cotan0, cotan1)):
        final = dot(keep, own_w[row]) + dot(came, other_w[row])
        results.append(jax.nn.gelu(final).astype(bf16))
        back_fn = jax.vjp(jax.nn.gelu, final)[1]
        grads.append(back_fn(cotan.astype(jnp.float32))[0].astype(bf16))

    terms = [None] * SECTIONS
    for section in (5, 4):
        own_w, other_w = full[section][0], full[section][1]
        sent = (dot_back(grads[0], other_w[0]) + dot_back(grads[1], other_w[1])).astype(bf16)
        back = flip(sent, section - 1)
        kept = (dot_back(grads[0], own_w[0]) + dot_back(grads[1], own_w[1])).astype(bf16)
        terms[section] = jnp.stack(
            [jnp.stack([dot_rows(part, grad) for grad in grads]) for part in inputs[section]]
        )
        grads = [kept, back]
    grad = jnp.stack(grads)
    for section in (3, 2, 1):
        own_w, other_w = full[section][0], full[section][1]
        sent = dot_back(grad, other_w).astype(bf16)
        back = flip(sent, section - 1)
        terms[section] = row_terms(inputs[section], grad)
        if section == 3:
            chip = chip_sum(jnp.stack(terms[3:]))
            parts_high = all_parts(chip)
        grad = (dot_back(grad, own_w) + back.astype(jnp.float32)).astype(bf16)
        if section == 2:
            grad = after(grad, chip)
    terms[0] = jnp.stack([dot_rows(part, grad) for part in inputs[0]])
    chip = after(chip_sum(jnp.stack(terms[:3])), parts_high)
    parts_low = all_parts(chip)

    out_came = flip(after(results[1], sent), 4)
    out_keep, out_send = jnp.where(same, results[0], out_came), jnp.where(same, out_came, results[0])
    out_came = flip(after(out_send, chip), 3)
    result = jnp.concatenate([jnp.where(low, out_came, out_keep), jnp.where(low, out_keep, out_came)], axis=1)

    rows = local(unorder_late, matchings, parts_high, outs=[shape(2, 2, 2, depth)])
    row0, row1 = rows[0], jnp.stack([rows[1, 0], flip(rows[1, 1], 4)])
    keep, send = jnp.where(same, row0, row1), jnp.where(same, row1, row0)
    came = flip(send, 3).reshape(4 * depth, width)
    weight_grad = local(
        finish, matchings, parts_low, parts_high, keep, came, outs=[shape(6, 2, 2, depth, dtype=jnp.float32)]
    )

    grad = after(grad, chip)
    own_w, other_w = full[0][0], full[0][1]
    first, second = [
        (dot_back(grad[r], own_w[r]) + dot_back(grad[1 - r], other_w[1 - r])).astype(bf16) for r in range(2)
    ]
    input_grad = jnp.concatenate([jnp.where(low, second, first), jnp.where(low, first, second)], axis=1)
    return result, input_grad, weight_grad


def solution(mesh):
    placed = (P("tok", "blk"), P(None, "blk", None, "tok", None), P(), P("tok", "blk"))
    return jax.shard_map(
        body,
        mesh=mesh,
        in_specs=placed,
        out_specs=(P("tok", "blk"), P("tok", "blk"), P(None, "blk", None, "tok", None)),
        check_vma=False,
    )
```

```python
import math

import jax
import jax.numpy as jnp
from jax import lax
from jax.experimental import pallas as pl
from jax.experimental.pallas import tpu as pltpu
from jax.sharding import PartitionSpec as P


SECTIONS = 6


def flip(value, bit):
    mask = 1 << bit
    pairs = [(source, source ^ mask) for source in range(lax.axis_size("blk"))]
    return lax.ppermute(value, "blk", pairs)


def after(value, other):
    start = (0,) * other.ndim
    probe = lax.slice(other, start, (1,) * (other.ndim - 1) + other.shape[-1:]).reshape(other.shape[-1])
    return jnp.where(probe != probe, jnp.zeros_like(value), value)


def dot(left, right):
    return jnp.einsum("...tk,...kl->...tl", left, right, preferred_element_type=jnp.float32)


def dot_back(left, right):
    return jnp.einsum("...tl,...kl->...tk", left, right, preferred_element_type=jnp.float32)


def dot_rows(left, right):
    return jnp.einsum("...tk,...tl->...kl", left, right, preferred_element_type=jnp.float32).astype(jnp.bfloat16)


def bits():
    index = lax.axis_index("blk")
    return index, (index >> 3) & 1, (index >> 4) & 1


def choice(matchings, section, row):
    index, low, high = bits()
    if section < 4:
        block = (row ^ low) + 2 * index
        turn = 0
    elif section == 4:
        block = low + 2 * (index & 7) + 16 * (row ^ high) + 32 * high
        turn = row ^ high ^ low
    else:
        block = low + 2 * (index & 7) + 16 * high + 32 * (row ^ high)
        turn = row
    return (matchings[section, block] != block).astype(jnp.int32) ^ turn


def order_early(matchings, weights, first, rest):
    _, low, _ = bits()
    for section in range(4):
        for row in range(2):
            at = choice(matchings, section, row)
            out = first.at[0] if section == 0 else rest.at[section - 1]
            out[0, row] = weights[section, row ^ low, at]
            out[1, row] = weights[section, row ^ low, 1 - at]


def pack_late(matchings, weights, cotangent, keep, packed):
    _, low, _ = bits()
    width = weights.shape[-1]
    depth = weights.shape[-2]
    for place in range(2):
        for both in range(2):
            keep[place, both] = weights[4 + place, low, both]
            packed[pl.ds((2 * place + both) * depth, depth)] = weights[4 + place, 1 - low, both]
    packed[4 * depth :] = jnp.where(low == 1, cotangent[:, :width], cotangent[:, width:])


def between(matchings, keep, came, cotangent, fourth, fifth, packed, cotan):
    _, low, high = bits()
    width = keep.shape[-1]
    depth = keep.shape[-2]
    same = low == high

    def came_at(place, both):
        return came[pl.ds(pl.multiple_of((2 * place + both) * depth, depth), depth)]

    for row in range(2):
        at = choice(matchings, 4, row)
        own = same if row == 0 else jnp.logical_not(same)
        for slot, both in enumerate((at, 1 - at)):
            fourth[slot, row] = jnp.where(own, keep[0, both], came_at(0, both))
    for both in range(2):
        mine5, yours5 = keep[1, both], came_at(1, both)
        fifth[both] = jnp.where(same, mine5, yours5)
        packed[pl.ds(both * depth, depth)] = jnp.where(same, yours5, mine5)
    cot_keep = jnp.where(low == 1, cotangent[:, width:], cotangent[:, :width])
    cot_came = came[4 * depth :]
    cotan[...] = jnp.where(same, cot_keep, cot_came)
    packed[2 * depth :] = jnp.where(same, cot_came, cot_keep)


def gather_late(matchings, fourth, fifth, came, late):
    depth = fourth.shape[-2]
    late[0] = fourth[...]
    for row in range(2):
        at = choice(matchings, 5, row)
        for slot, both in enumerate((at, 1 - at)):
            if row == 0:
                late[1, slot, row] = fifth[both]
            else:
                late[1, slot, row] = came[pl.ds(pl.multiple_of(both * depth, depth), depth)]


def total(parts, place, slot, row):
    parts = [parts[chip, place, slot, row].astype(jnp.float32) for chip in range(parts.shape[0])]
    while len(parts) > 1:
        parts = [a + b for a, b in zip(parts[::2], parts[1::2])]
    return parts[0]


def unorder_late(matchings, parts, rows):
    for place in range(2):
        for row in range(2):
            at = choice(matchings, 4 + place, row)
            for slot, both in enumerate((at, 1 - at)):
                rows[row, place, both] = total(parts, 1 + place, slot, row).astype(rows.dtype)


def finish(matchings, parts_low, parts_high, keep, came, out):
    _, low, _ = bits()
    depth = out.shape[-2]
    for section in range(4):
        parts = parts_low if section < 3 else parts_high
        for row in range(2):
            at = choice(matchings, section, row)
            for slot, both in enumerate((at, 1 - at)):
                out[section, row ^ low, both] = total(parts, section % 3, slot, row)
    for place in range(2):
        for both in range(2):
            out[4 + place, low, both] = keep[place, both].astype(jnp.float32)
            given = came[pl.ds((2 * place + both) * depth, depth)]
            out[4 + place, 1 - low, both] = given.astype(jnp.float32)


def local(kernel, matchings, *arrays, outs):
    whole = pl.BlockSpec(memory_space=pltpu.VMEM)
    moved = sum(math.prod(x.shape) * x.dtype.itemsize for x in (*arrays, *outs))
    result = pl.pallas_call(
        kernel,
        out_shape=outs,
        in_specs=[pl.BlockSpec(memory_space=pltpu.SMEM)] + [whole] * len(arrays),
        out_specs=[whole] * len(outs),
        cost_estimate=pl.CostEstimate(flops=0, bytes_accessed=moved, transcendentals=0),
        compiler_params=pltpu.CompilerParams(vmem_limit_bytes=16 * 2**20),
    )(matchings, *arrays)
    return result[0] if len(outs) == 1 else result


def core_half(terms, core):
    count, both, per_dev, size, depth, width = terms.shape
    parts = terms.reshape(count, both, per_dev, size // 2, 2, depth, width)
    half = jnp.where(core == 1, parts[:, :, :, :, 1], parts[:, :, :, :, 0])
    return jnp.moveaxis(half, 3, 0)


def chip_sum(terms):
    count, both, per_dev, depth, width = terms.shape
    size = lax.axis_size("tok")
    core = lax.axis_index("tok") & 1
    terms = terms.reshape(count, both, per_dev, size, depth // size, width)
    came = lax.ppermute(core_half(terms, 1 - core), "tok", [(source, source ^ 1) for source in range(size)])
    return (core_half(terms, core).astype(jnp.float32) + came.astype(jnp.float32)).astype(jnp.bfloat16)


def all_parts(chip):
    size = lax.axis_size("tok")
    groups = [list(range(c, size, 2)) for c in range(2)]
    return lax.all_to_all(chip, "tok", 0, 0, axis_index_groups=groups)


def body(activations, weights, matchings, cotangent):
    depth, width = weights.shape[3:]
    tokens = activations.shape[0]
    bf16 = jnp.bfloat16
    _, low, high = bits()
    low, same = low == 1, low == high

    def shape(*dims, dtype=bf16):
        return jax.ShapeDtypeStruct((*dims, width), dtype)

    first, rest = local(order_early, matchings, weights, outs=[shape(1, 2, 2, depth), shape(3, 2, 2, depth)])
    keep, packed = local(
        pack_late, matchings, weights, cotangent, outs=[shape(2, 2, depth), shape(4 * depth + tokens)]
    )
    came = flip(packed, 3)
    full = list(lax.all_gather(first, "tok", axis=3, tiled=True))
    full += list(lax.all_gather(rest, "tok", axis=3, tiled=True))

    left, right = activations[:, :width], activations[:, width:]
    value = jnp.stack([jnp.where(low, right, left), jnp.where(low, left, right)])
    other = value[::-1]
    inputs = [(value, other)]
    value = (dot(value, full[0][0]) + dot(other, full[0][1])).astype(bf16)

    fourth, fifth, packed, cotan0 = local(
        between,
        matchings,
        keep,
        came,
        cotangent,
        outs=[shape(2, 2, depth), shape(2, depth), shape(2 * depth + tokens), shape(tokens)],
    )
    came = flip(packed, 4)
    cotan1 = came[2 * depth :]
    late = local(gather_late, matchings, fourth, fifth, came, outs=[shape(2, 2, 2, depth)])
    full += list(lax.all_gather(late, "tok", axis=3, tiled=True))

    for section in range(1, 4):
        other = flip(value, section - 1)
        inputs.append((value, other))
        full[section] = after(full[section], value)
        own_w, other_w = full[section][0], full[section][1]
        if section < 3:
            value = (dot(value, own_w) + dot(other, other_w)).astype(bf16)
        else:
            send = (dot(value[1], own_w[1]) + dot(other[1], other_w[1])).astype(bf16)
            keep = (dot(value[0], own_w[0]) + dot(other[0], other_w[0])).astype(bf16)
    came = flip(send, 3)
    inputs.append((keep, came))
    full[4] = after(full[4], send)
    own_w, other_w = full[4][0], full[4][1]
    send = (dot(keep, own_w[1]) + dot(came, other_w[1])).astype(bf16)
    keep = (dot(keep, own_w[0]) + dot(came, other_w[0])).astype(bf16)
    came = flip(send, 4)
    inputs.append((keep, came))
    full[5] = after(full[5], send)
    own_w, other_w = full[5][0], full[5][1]

    results, grads = [], []
    for row, cotan in enumerate((cotan0, cotan1)):
        final = dot(keep, own_w[row]) + dot(came, other_w[row])
        results.append(jax.nn.gelu(final).astype(bf16))
        back_fn = jax.vjp(jax.nn.gelu, final)[1]
        grads.append(back_fn(cotan.astype(jnp.float32))[0].astype(bf16))

    terms = [None] * SECTIONS
    for section in (5, 4):
        own_w, other_w = full[section][0], full[section][1]
        sent = (dot_back(grads[0], other_w[0]) + dot_back(grads[1], other_w[1])).astype(bf16)
        back = flip(sent, section - 1)
        if section == 5:
            grads = [after(grad, sent) for grad in grads]
        kept = (dot_back(grads[0], own_w[0]) + dot_back(grads[1], own_w[1])).astype(bf16)
        terms[section] = jnp.stack(
            [jnp.stack([dot_rows(part, grad) for grad in grads]) for part in inputs[section]]
        )
        grads = [kept, back]
    grad = jnp.stack(grads)
    for section in (3, 2, 1):
        own_w, other_w = full[section][0], full[section][1]
        sent = dot_back(grad, other_w).astype(bf16)
        back = flip(sent, section - 1)
        terms[section] = jnp.stack([dot_rows(part, grad) for part in inputs[section]])
        if section == 3:
            chip = chip_sum(jnp.stack(terms[3:]))
            parts_high = all_parts(chip)
        grad = (dot_back(grad, own_w) + back.astype(jnp.float32)).astype(bf16)
        if section == 2:
            grad = after(grad, chip)
    terms[0] = jnp.stack([dot_rows(part, grad) for part in inputs[0]])
    chip = after(chip_sum(jnp.stack(terms[:3])), parts_high)
    parts_low = all_parts(chip)

    out_came = flip(results[1], 4)
    out_keep, out_send = jnp.where(same, results[0], out_came), jnp.where(same, out_came, results[0])
    out_came = flip(after(out_send, chip), 3)
    result = jnp.concatenate([jnp.where(low, out_came, out_keep), jnp.where(low, out_keep, out_came)], axis=1)

    rows = local(unorder_late, matchings, parts_high, outs=[shape(2, 2, 2, depth)])
    row0, row1 = rows[0], jnp.stack([rows[1, 0], flip(rows[1, 1], 4)])
    keep, send = jnp.where(same, row0, row1), jnp.where(same, row1, row0)
    came = flip(send, 3).reshape(4 * depth, width)
    weight_grad = local(
        finish, matchings, parts_low, parts_high, keep, came, outs=[shape(6, 2, 2, depth, dtype=jnp.float32)]
    )

    grad = after(grad, chip)
    own_w, other_w = full[0][0], full[0][1]
    first, second = [
        (dot_back(grad[r], own_w[r]) + dot_back(grad[1 - r], other_w[1 - r])).astype(bf16) for r in range(2)
    ]
    input_grad = jnp.concatenate([jnp.where(low, second, first), jnp.where(low, first, second)], axis=1)
    return result, input_grad, weight_grad


def solution(mesh):
    placed = (P("tok", "blk"), P(None, "blk", None, "tok", None), P(), P("tok", "blk"))
    return jax.shard_map(
        body,
        mesh=mesh,
        in_specs=placed,
        out_specs=(P("tok", "blk"), P("tok", "blk"), P(None, "blk", None, "tok", None)),
        check_vma=False,
    )
```

```python
import math

import jax
import jax.numpy as jnp
from jax import lax
from jax.experimental import pallas as pl
from jax.experimental.pallas import tpu as pltpu
from jax.sharding import PartitionSpec as P


SECTIONS = 6


def flip(value, bit):
    mask = 1 << bit
    pairs = [(source, source ^ mask) for source in range(lax.axis_size("blk"))]
    return lax.ppermute(value, "blk", pairs)


def after(value, other):
    start = (0,) * other.ndim
    probe = lax.slice(other, start, (1,) * (other.ndim - 1) + other.shape[-1:]).reshape(other.shape[-1])
    return jnp.where(probe != probe, jnp.zeros_like(value), value)


def dot(left, right):
    return jnp.einsum("...tk,...kl->...tl", left, right, preferred_element_type=jnp.float32)


def dot_back(left, right):
    return jnp.einsum("...tl,...kl->...tk", left, right, preferred_element_type=jnp.float32)


def dot_rows(left, right):
    return jnp.einsum("...tk,...tl->...kl", left, right, preferred_element_type=jnp.float32).astype(jnp.bfloat16)


def bits():
    index = lax.axis_index("blk")
    return index, (index >> 3) & 1, (index >> 4) & 1


def choice(matchings, section, row):
    index, low, high = bits()
    if section < 4:
        block = (row ^ low) + 2 * index
        turn = 0
    elif section == 4:
        block = low + 2 * (index & 7) + 16 * (row ^ high) + 32 * high
        turn = row ^ high ^ low
    else:
        block = low + 2 * (index & 7) + 16 * high + 32 * (row ^ high)
        turn = row
    return (matchings[section, block] != block).astype(jnp.int32) ^ turn


def order_early(matchings, weights, first, rest, keep, send):
    _, low, _ = bits()
    depth = weights.shape[-2]
    for section in range(4):
        for row in range(2):
            at = choice(matchings, section, row)
            out = first.at[0] if section == 0 else rest.at[section - 1]
            out[0, row] = weights[section, row ^ low, at]
            out[1, row] = weights[section, row ^ low, 1 - at]
    for place in range(2):
        for both in range(2):
            keep[place, both] = weights[4 + place, low, both]
            send[pl.ds((2 * place + both) * depth, depth)] = weights[4 + place, 1 - low, both]


def pack_late(send, cotangent, packed):
    _, low, _ = bits()
    rows, width = send.shape
    packed[:rows] = send[...]
    packed[rows:] = jnp.where(low == 1, cotangent[:, :width], cotangent[:, width:])


def between(matchings, keep, came, cotangent, fourth, fifth, packed, cotan):
    _, low, high = bits()
    width = keep.shape[-1]
    depth = keep.shape[-2]
    same = low == high

    def came_at(place, both):
        return came[pl.ds(pl.multiple_of((2 * place + both) * depth, depth), depth)]

    for row in range(2):
        at = choice(matchings, 4, row)
        own = same if row == 0 else jnp.logical_not(same)
        for slot, both in enumerate((at, 1 - at)):
            fourth[slot, row] = jnp.where(own, keep[0, both], came_at(0, both))
    for both in range(2):
        mine5, yours5 = keep[1, both], came_at(1, both)
        fifth[both] = jnp.where(same, mine5, yours5)
        packed[pl.ds(both * depth, depth)] = jnp.where(same, yours5, mine5)
    cot_keep = jnp.where(low == 1, cotangent[:, width:], cotangent[:, :width])
    cot_came = came[4 * depth :]
    cotan[...] = jnp.where(same, cot_keep, cot_came)
    packed[2 * depth :] = jnp.where(same, cot_came, cot_keep)


def gather_late(matchings, fourth, fifth, came, late):
    depth = fourth.shape[-2]
    late[0] = fourth[...]
    for row in range(2):
        at = choice(matchings, 5, row)
        for slot, both in enumerate((at, 1 - at)):
            if row == 0:
                late[1, slot, row] = fifth[both]
            else:
                late[1, slot, row] = came[pl.ds(pl.multiple_of(both * depth, depth), depth)]


def total(parts, place, slot, row):
    parts = [parts[chip, place, slot, row].astype(jnp.float32) for chip in range(parts.shape[0])]
    while len(parts) > 1:
        parts = [a + b for a, b in zip(parts[::2], parts[1::2])]
    return parts[0]


def unorder_late(matchings, parts, rows):
    for place in range(2):
        for row in range(2):
            at = choice(matchings, 4 + place, row)
            for slot, both in enumerate((at, 1 - at)):
                rows[row, place, both] = total(parts, 1 + place, slot, row).astype(rows.dtype)


def finish(matchings, parts_low, parts_high, keep, came, out):
    _, low, _ = bits()
    depth = out.shape[-2]
    for section in range(4):
        parts = parts_low if section < 3 else parts_high
        for row in range(2):
            at = choice(matchings, section, row)
            for slot, both in enumerate((at, 1 - at)):
                out[section, row ^ low, both] = total(parts, section % 3, slot, row)
    for place in range(2):
        for both in range(2):
            out[4 + place, low, both] = keep[place, both].astype(jnp.float32)
            given = came[pl.ds((2 * place + both) * depth, depth)]
            out[4 + place, 1 - low, both] = given.astype(jnp.float32)


def local(kernel, matchings, *arrays, outs):
    whole = pl.BlockSpec(memory_space=pltpu.VMEM)
    scalars = () if matchings is None else (matchings,)
    moved = sum(math.prod(x.shape) * x.dtype.itemsize for x in (*arrays, *outs))
    result = pl.pallas_call(
        kernel,
        out_shape=outs,
        in_specs=[pl.BlockSpec(memory_space=pltpu.SMEM)] * len(scalars) + [whole] * len(arrays),
        out_specs=[whole] * len(outs),
        cost_estimate=pl.CostEstimate(flops=0, bytes_accessed=moved, transcendentals=0),
        compiler_params=pltpu.CompilerParams(vmem_limit_bytes=16 * 2**20),
    )(*scalars, *arrays)
    return result[0] if len(outs) == 1 else result


def core_half(terms, core):
    count, both, per_dev, size, depth, width = terms.shape
    parts = terms.reshape(count, both, per_dev, size // 2, 2, depth, width)
    half = jnp.where(core == 1, parts[:, :, :, :, 1], parts[:, :, :, :, 0])
    return jnp.moveaxis(half, 3, 0)


def chip_sum(terms):
    count, both, per_dev, depth, width = terms.shape
    size = lax.axis_size("tok")
    core = lax.axis_index("tok") & 1
    terms = terms.reshape(count, both, per_dev, size, depth // size, width)
    came = lax.ppermute(core_half(terms, 1 - core), "tok", [(source, source ^ 1) for source in range(size)])
    return (core_half(terms, core).astype(jnp.float32) + came.astype(jnp.float32)).astype(jnp.bfloat16)


def all_parts(chip):
    size = lax.axis_size("tok")
    groups = [list(range(c, size, 2)) for c in range(2)]
    return lax.all_to_all(chip, "tok", 0, 0, axis_index_groups=groups)


def body(activations, weights, matchings, cotangent):
    depth, width = weights.shape[3:]
    tokens = activations.shape[0]
    bf16 = jnp.bfloat16
    _, low, high = bits()
    low, same = low == 1, low == high

    def shape(*dims, dtype=bf16):
        return jax.ShapeDtypeStruct((*dims, width), dtype)

    first, rest, keep, send = local(
        order_early,
        matchings,
        weights,
        outs=[shape(1, 2, 2, depth), shape(3, 2, 2, depth), shape(2, 2, depth), shape(4 * depth)],
    )
    packed = local(pack_late, None, send, cotangent, outs=[shape(4 * depth + tokens)])
    came = flip(packed, 3)
    full = list(lax.all_gather(first, "tok", axis=3, tiled=True))
    full += list(lax.all_gather(rest, "tok", axis=3, tiled=True))

    left, right = activations[:, :width], activations[:, width:]
    value = jnp.stack([jnp.where(low, right, left), jnp.where(low, left, right)])
    other = value[::-1]
    inputs = [(value, other)]
    value = (dot(value, full[0][0]) + dot(other, full[0][1])).astype(bf16)

    fourth, fifth, packed, cotan0 = local(
        between,
        matchings,
        keep,
        came,
        cotangent,
        outs=[shape(2, 2, depth), shape(2, depth), shape(2 * depth + tokens), shape(tokens)],
    )
    came = flip(packed, 4)
    cotan1 = came[2 * depth :]
    late = local(gather_late, matchings, fourth, fifth, came, outs=[shape(2, 2, 2, depth)])
    full += list(lax.all_gather(late, "tok", axis=3, tiled=True))

    for section in range(1, 4):
        other = flip(value, section - 1)
        inputs.append((value, other))
        full[section] = after(full[section], value)
        own_w, other_w = full[section][0], full[section][1]
        if section < 3:
            value = (dot(value, own_w) + dot(other, other_w)).astype(bf16)
        else:
            send = (dot(value[1], own_w[1]) + dot(other[1], other_w[1])).astype(bf16)
            keep = (dot(value[0], own_w[0]) + dot(other[0], other_w[0])).astype(bf16)
    came = flip(send, 3)
    inputs.append((keep, came))
    full[4] = after(full[4], send)
    own_w, other_w = full[4][0], full[4][1]
    send = (dot(keep, own_w[1]) + dot(came, other_w[1])).astype(bf16)
    keep = (dot(keep, own_w[0]) + dot(came, other_w[0])).astype(bf16)
    came = flip(send, 4)
    inputs.append((keep, came))
    full[5] = after(full[5], send)
    own_w, other_w = full[5][0], full[5][1]

    results, grads = [], []
    for row, cotan in enumerate((cotan0, cotan1)):
        final = dot(keep, own_w[row]) + dot(came, other_w[row])
        results.append(jax.nn.gelu(final).astype(bf16))
        back_fn = jax.vjp(jax.nn.gelu, final)[1]
        grads.append(back_fn(cotan.astype(jnp.float32))[0].astype(bf16))

    terms = [None] * SECTIONS
    for section in (5, 4):
        own_w, other_w = full[section][0], full[section][1]
        sent = (dot_back(grads[0], other_w[0]) + dot_back(grads[1], other_w[1])).astype(bf16)
        back = flip(sent, section - 1)
        if section == 5:
            grads = [after(grad, sent) for grad in grads]
        kept = (dot_back(grads[0], own_w[0]) + dot_back(grads[1], own_w[1])).astype(bf16)
        terms[section] = jnp.stack(
            [jnp.stack([dot_rows(part, grad) for grad in grads]) for part in inputs[section]]
        )
        grads = [kept, back]
    grad = jnp.stack(grads)
    for section in (3, 2, 1):
        own_w, other_w = full[section][0], full[section][1]
        sent = dot_back(grad, other_w).astype(bf16)
        back = flip(sent, section - 1)
        terms[section] = jnp.stack([dot_rows(part, grad) for part in inputs[section]])
        if section == 3:
            chip = chip_sum(jnp.stack(terms[3:]))
            parts_high = all_parts(chip)
        grad = (dot_back(grad, own_w) + back.astype(jnp.float32)).astype(bf16)
        if section == 2:
            grad = after(grad, chip)
    terms[0] = jnp.stack([dot_rows(part, grad) for part in inputs[0]])
    chip = after(chip_sum(jnp.stack(terms[:3])), parts_high)
    parts_low = all_parts(chip)

    out_came = flip(results[1], 4)
    out_keep, out_send = jnp.where(same, results[0], out_came), jnp.where(same, out_came, results[0])
    out_came = flip(after(out_send, chip), 3)
    result = jnp.concatenate([jnp.where(low, out_came, out_keep), jnp.where(low, out_keep, out_came)], axis=1)

    rows = local(unorder_late, matchings, parts_high, outs=[shape(2, 2, 2, depth)])
    row0, row1 = rows[0], jnp.stack([rows[1, 0], flip(rows[1, 1], 4)])
    keep, send = jnp.where(same, row0, row1), jnp.where(same, row1, row0)
    came = flip(send, 3).reshape(4 * depth, width)
    weight_grad = local(
        finish, matchings, parts_low, parts_high, keep, came, outs=[shape(6, 2, 2, depth, dtype=jnp.float32)]
    )

    grad = after(grad, chip)
    own_w, other_w = full[0][0], full[0][1]
    first, second = [
        (dot_back(grad[r], own_w[r]) + dot_back(grad[1 - r], other_w[1 - r])).astype(bf16) for r in range(2)
    ]
    input_grad = jnp.concatenate([jnp.where(low, second, first), jnp.where(low, first, second)], axis=1)
    return result, input_grad, weight_grad


def solution(mesh):
    placed = (P("tok", "blk"), P(None, "blk", None, "tok", None), P(), P("tok", "blk"))
    return jax.shard_map(
        body,
        mesh=mesh,
        in_specs=placed,
        out_specs=(P("tok", "blk"), P("tok", "blk"), P(None, "blk", None, "tok", None)),
        check_vma=False,
    )
```

```python
import math

import jax
import jax.numpy as jnp
from jax import lax
from jax.experimental import pallas as pl
from jax.experimental.pallas import tpu as pltpu
from jax.sharding import PartitionSpec as P


SECTIONS = 6


def flip(value, bit):
    mask = 1 << bit
    pairs = [(source, source ^ mask) for source in range(lax.axis_size("blk"))]
    return lax.ppermute(value, "blk", pairs)


def after(value, other):
    start = (0,) * other.ndim
    probe = lax.slice(other, start, (1,) * (other.ndim - 1) + other.shape[-1:]).reshape(other.shape[-1])
    return jnp.where(probe != probe, jnp.zeros_like(value), value)


def dot(left, right):
    return jnp.einsum("...tk,...kl->...tl", left, right, preferred_element_type=jnp.float32)


def dot_back(left, right):
    return jnp.einsum("...tl,...kl->...tk", left, right, preferred_element_type=jnp.float32)


def dot_rows(left, right):
    return jnp.einsum("...tk,...tl->...kl", left, right, preferred_element_type=jnp.float32).astype(jnp.bfloat16)


def bits():
    index = lax.axis_index("blk")
    return index, (index >> 3) & 1, (index >> 4) & 1


def choice(matchings, section, row):
    index, low, high = bits()
    if section < 4:
        block = (row ^ low) + 2 * index
        turn = 0
    elif section == 4:
        block = low + 2 * (index & 7) + 16 * (row ^ high) + 32 * high
        turn = row ^ high ^ low
    else:
        block = low + 2 * (index & 7) + 16 * high + 32 * (row ^ high)
        turn = row
    return (matchings[section, block] != block).astype(jnp.int32) ^ turn


def order_early(matchings, weights, first, rest, keep, send):
    _, low, _ = bits()
    depth = weights.shape[-2]
    for section in range(4):
        for row in range(2):
            at = choice(matchings, section, row)
            out = first.at[0] if section == 0 else rest.at[section - 1]
            out[0, row] = weights[section, row ^ low, at]
            out[1, row] = weights[section, row ^ low, 1 - at]
    for place in range(2):
        for both in range(2):
            keep[place, both] = weights[4 + place, low, both]
            send[pl.ds((2 * place + both) * depth, depth)] = weights[4 + place, 1 - low, both]


def pack_late(send, cotangent, packed):
    _, low, _ = bits()
    rows, width = send.shape
    packed[:rows] = send[...]
    packed[rows:] = jnp.where(low == 1, cotangent[:, :width], cotangent[:, width:])


def between(matchings, keep, came, cotangent, fourth, fifth, send, cotan, cot_send):
    _, low, high = bits()
    width = keep.shape[-1]
    depth = keep.shape[-2]
    same = low == high

    def came_at(place, both):
        return came[pl.ds(pl.multiple_of((2 * place + both) * depth, depth), depth)]

    for row in range(2):
        at = choice(matchings, 4, row)
        own = same if row == 0 else jnp.logical_not(same)
        for slot, both in enumerate((at, 1 - at)):
            fourth[slot, row] = jnp.where(own, keep[0, both], came_at(0, both))
    for both in range(2):
        mine5, yours5 = keep[1, both], came_at(1, both)
        fifth[both] = jnp.where(same, mine5, yours5)
        send[both] = jnp.where(same, yours5, mine5)
    cot_keep = jnp.where(low == 1, cotangent[:, width:], cotangent[:, :width])
    cot_came = came[4 * depth :]
    cotan[...] = jnp.where(same, cot_keep, cot_came)
    cot_send[...] = jnp.where(same, cot_came, cot_keep)


def gather_late(matchings, fourth, fifth, came, late):
    depth = fourth.shape[-2]
    late[0] = fourth[...]
    for row in range(2):
        at = choice(matchings, 5, row)
        for slot, both in enumerate((at, 1 - at)):
            if row == 0:
                late[1, slot, row] = fifth[both]
            else:
                late[1, slot, row] = came[both]


def total(parts, place, slot, row):
    parts = [parts[chip, place, slot, row].astype(jnp.float32) for chip in range(parts.shape[0])]
    while len(parts) > 1:
        parts = [a + b for a, b in zip(parts[::2], parts[1::2])]
    return parts[0]


def unorder_late(matchings, parts, rows):
    for place in range(2):
        for row in range(2):
            at = choice(matchings, 4 + place, row)
            for slot, both in enumerate((at, 1 - at)):
                rows[row, place, both] = total(parts, 1 + place, slot, row).astype(rows.dtype)


def finish(matchings, parts_low, parts_high, keep, came, out):
    _, low, _ = bits()
    depth = out.shape[-2]
    for section in range(4):
        parts = parts_low if section < 3 else parts_high
        for row in range(2):
            at = choice(matchings, section, row)
            for slot, both in enumerate((at, 1 - at)):
                out[section, row ^ low, both] = total(parts, section % 3, slot, row)
    for place in range(2):
        for both in range(2):
            out[4 + place, low, both] = keep[place, both].astype(jnp.float32)
            given = came[pl.ds((2 * place + both) * depth, depth)]
            out[4 + place, 1 - low, both] = given.astype(jnp.float32)


def local(kernel, matchings, *arrays, outs):
    whole = pl.BlockSpec(memory_space=pltpu.VMEM)
    scalars = () if matchings is None else (matchings,)
    moved = sum(math.prod(x.shape) * x.dtype.itemsize for x in (*arrays, *outs))
    result = pl.pallas_call(
        kernel,
        out_shape=outs,
        in_specs=[pl.BlockSpec(memory_space=pltpu.SMEM)] * len(scalars) + [whole] * len(arrays),
        out_specs=[whole] * len(outs),
        cost_estimate=pl.CostEstimate(flops=0, bytes_accessed=moved, transcendentals=0),
        compiler_params=pltpu.CompilerParams(vmem_limit_bytes=16 * 2**20),
    )(*scalars, *arrays)
    return result[0] if len(outs) == 1 else result


def core_half(terms, core):
    count, both, per_dev, size, depth, width = terms.shape
    parts = terms.reshape(count, both, per_dev, size // 2, 2, depth, width)
    half = jnp.where(core == 1, parts[:, :, :, :, 1], parts[:, :, :, :, 0])
    return jnp.moveaxis(half, 3, 0)


def chip_sum(terms):
    count, both, per_dev, depth, width = terms.shape
    size = lax.axis_size("tok")
    core = lax.axis_index("tok") & 1
    terms = terms.reshape(count, both, per_dev, size, depth // size, width)
    came = lax.ppermute(core_half(terms, 1 - core), "tok", [(source, source ^ 1) for source in range(size)])
    return (core_half(terms, core).astype(jnp.float32) + came.astype(jnp.float32)).astype(jnp.bfloat16)


def all_parts(chip):
    size = lax.axis_size("tok")
    groups = [list(range(c, size, 2)) for c in range(2)]
    return lax.all_to_all(chip, "tok", 0, 0, axis_index_groups=groups)


def body(activations, weights, matchings, cotangent):
    depth, width = weights.shape[3:]
    tokens = activations.shape[0]
    bf16 = jnp.bfloat16
    _, low, high = bits()
    low, same = low == 1, low == high

    def shape(*dims, dtype=bf16):
        return jax.ShapeDtypeStruct((*dims, width), dtype)

    first, rest, keep, send = local(
        order_early,
        matchings,
        weights,
        outs=[shape(1, 2, 2, depth), shape(3, 2, 2, depth), shape(2, 2, depth), shape(4 * depth)],
    )
    packed = local(pack_late, None, send, cotangent, outs=[shape(4 * depth + tokens)])
    came = flip(packed, 3)
    full = list(lax.all_gather(first, "tok", axis=3, tiled=True))
    full += list(lax.all_gather(rest, "tok", axis=3, tiled=True))

    left, right = activations[:, :width], activations[:, width:]
    value = jnp.stack([jnp.where(low, right, left), jnp.where(low, left, right)])
    other = value[::-1]
    inputs = [(value, other)]
    value = (dot(value, full[0][0]) + dot(other, full[0][1])).astype(bf16)

    fourth, fifth, send, cotan0, cot_send = local(
        between,
        matchings,
        keep,
        came,
        cotangent,
        outs=[shape(2, 2, depth), shape(2, depth), shape(2, depth), shape(tokens), shape(tokens)],
    )
    came = flip(send, 4)
    cotan1 = flip(cot_send, 4)
    late = local(gather_late, matchings, fourth, fifth, came, outs=[shape(2, 2, 2, depth)])
    full += list(lax.all_gather(late, "tok", axis=3, tiled=True))

    for section in range(1, 4):
        other = flip(value, section - 1)
        inputs.append((value, other))
        full[section] = after(full[section], value)
        own_w, other_w = full[section][0], full[section][1]
        if section < 3:
            value = (dot(value, own_w) + dot(other, other_w)).astype(bf16)
            if section == 1:
                value = after(value, cotan1)
        else:
            send = (dot(value[1], own_w[1]) + dot(other[1], other_w[1])).astype(bf16)
            keep = (dot(value[0], own_w[0]) + dot(other[0], other_w[0])).astype(bf16)
    came = flip(send, 3)
    inputs.append((keep, came))
    full[4] = after(full[4], send)
    own_w, other_w = full[4][0], full[4][1]
    send = (dot(keep, own_w[1]) + dot(came, other_w[1])).astype(bf16)
    keep = (dot(keep, own_w[0]) + dot(came, other_w[0])).astype(bf16)
    came = flip(send, 4)
    inputs.append((keep, came))
    full[5] = after(full[5], send)
    own_w, other_w = full[5][0], full[5][1]

    results, grads = [], []
    for row, cotan in enumerate((cotan0, cotan1)):
        final = dot(keep, own_w[row]) + dot(came, other_w[row])
        results.append(jax.nn.gelu(final).astype(bf16))
        back_fn = jax.vjp(jax.nn.gelu, final)[1]
        grads.append(back_fn(cotan.astype(jnp.float32))[0].astype(bf16))

    terms = [None] * SECTIONS
    for section in (5, 4):
        own_w, other_w = full[section][0], full[section][1]
        sent = (dot_back(grads[0], other_w[0]) + dot_back(grads[1], other_w[1])).astype(bf16)
        back = flip(sent, section - 1)
        if section == 5:
            grads = [after(grad, sent) for grad in grads]
        kept = (dot_back(grads[0], own_w[0]) + dot_back(grads[1], own_w[1])).astype(bf16)
        terms[section] = jnp.stack(
            [jnp.stack([dot_rows(part, grad) for grad in grads]) for part in inputs[section]]
        )
        grads = [kept, back]
    grad = jnp.stack(grads)
    for section in (3, 2, 1):
        own_w, other_w = full[section][0], full[section][1]
        sent = dot_back(grad, other_w).astype(bf16)
        back = flip(sent, section - 1)
        terms[section] = jnp.stack([dot_rows(part, grad) for part in inputs[section]])
        if section == 3:
            chip = chip_sum(jnp.stack(terms[3:]))
            parts_high = all_parts(chip)
        grad = (dot_back(grad, own_w) + back.astype(jnp.float32)).astype(bf16)
        if section == 2:
            grad = after(grad, chip)
    terms[0] = jnp.stack([dot_rows(part, grad) for part in inputs[0]])
    chip = after(chip_sum(jnp.stack(terms[:3])), parts_high)
    parts_low = all_parts(chip)

    out_came = flip(results[1], 4)
    out_keep, out_send = jnp.where(same, results[0], out_came), jnp.where(same, out_came, results[0])
    out_came = flip(after(out_send, chip), 3)
    result = jnp.concatenate([jnp.where(low, out_came, out_keep), jnp.where(low, out_keep, out_came)], axis=1)

    rows = local(unorder_late, matchings, parts_high, outs=[shape(2, 2, 2, depth)])
    row0, row1 = rows[0], jnp.stack([rows[1, 0], flip(rows[1, 1], 4)])
    keep, send = jnp.where(same, row0, row1), jnp.where(same, row1, row0)
    came = flip(send, 3).reshape(4 * depth, width)
    weight_grad = local(
        finish, matchings, parts_low, parts_high, keep, came, outs=[shape(6, 2, 2, depth, dtype=jnp.float32)]
    )

    grad = after(grad, chip)
    own_w, other_w = full[0][0], full[0][1]
    first, second = [
        (dot_back(grad[r], own_w[r]) + dot_back(grad[1 - r], other_w[1 - r])).astype(bf16) for r in range(2)
    ]
    input_grad = jnp.concatenate([jnp.where(low, second, first), jnp.where(low, first, second)], axis=1)
    return result, input_grad, weight_grad


def solution(mesh):
    placed = (P("tok", "blk"), P(None, "blk", None, "tok", None), P(), P("tok", "blk"))
    return jax.shard_map(
        body,
        mesh=mesh,
        in_specs=placed,
        out_specs=(P("tok", "blk"), P("tok", "blk"), P(None, "blk", None, "tok", None)),
        check_vma=False,
    )
```

```python
import math

import jax
import jax.numpy as jnp
from jax import lax
from jax.experimental import pallas as pl
from jax.experimental.pallas import tpu as pltpu
from jax.sharding import PartitionSpec as P


SECTIONS = 6


def flip(value, bit):
    mask = 1 << bit
    pairs = [(source, source ^ mask) for source in range(lax.axis_size("blk"))]
    return lax.ppermute(value, "blk", pairs)


def after(value, other):
    start = (0,) * other.ndim
    probe = lax.slice(other, start, (1,) * (other.ndim - 1) + other.shape[-1:]).reshape(other.shape[-1])
    return jnp.where(probe != probe, jnp.zeros_like(value), value)


def dot(left, right):
    return jnp.einsum("...tk,...kl->...tl", left, right, preferred_element_type=jnp.float32)


def dot_back(left, right):
    return jnp.einsum("...tl,...kl->...tk", left, right, preferred_element_type=jnp.float32)


def dot_rows(left, right):
    return jnp.einsum("...tk,...tl->...kl", left, right, preferred_element_type=jnp.float32).astype(jnp.bfloat16)


def bits():
    index = lax.axis_index("blk")
    return index, (index >> 3) & 1, (index >> 4) & 1


def choice(matchings, section, row):
    index, low, high = bits()
    if section < 4:
        block = (row ^ low) + 2 * index
        turn = 0
    elif section == 4:
        block = low + 2 * (index & 7) + 16 * (row ^ high) + 32 * high
        turn = row ^ high ^ low
    else:
        block = low + 2 * (index & 7) + 16 * high + 32 * (row ^ high)
        turn = row
    return (matchings[section, block] != block).astype(jnp.int32) ^ turn


def order_early(matchings, weights, first, rest, keep, send):
    _, low, _ = bits()
    depth = weights.shape[-2]
    for section in range(4):
        for row in range(2):
            at = choice(matchings, section, row)
            out = first.at[0] if section == 0 else rest.at[section - 1]
            out[0, row] = weights[section, row ^ low, at]
            out[1, row] = weights[section, row ^ low, 1 - at]
    for place in range(2):
        for both in range(2):
            keep[place, both] = weights[4 + place, low, both]
            send[pl.ds((2 * place + both) * depth, depth)] = weights[4 + place, 1 - low, both]


def pack_late(send, cotangent, packed):
    _, low, _ = bits()
    rows, width = send.shape
    packed[:rows] = send[...]
    packed[rows:] = jnp.where(low == 1, cotangent[:, :width], cotangent[:, width:])


def between(matchings, keep, came, cotangent, fourth, fifth, packed, cotan):
    _, low, high = bits()
    width = keep.shape[-1]
    depth = keep.shape[-2]
    same = low == high

    def came_at(place, both):
        return came[pl.ds(pl.multiple_of((2 * place + both) * depth, depth), depth)]

    for row in range(2):
        at = choice(matchings, 4, row)
        own = same if row == 0 else jnp.logical_not(same)
        for slot, both in enumerate((at, 1 - at)):
            fourth[slot, row] = jnp.where(own, keep[0, both], came_at(0, both))
    for both in range(2):
        mine5, yours5 = keep[1, both], came_at(1, both)
        fifth[both] = jnp.where(same, mine5, yours5)
        packed[pl.ds(both * depth, depth)] = jnp.where(same, yours5, mine5)
    cot_keep = jnp.where(low == 1, cotangent[:, width:], cotangent[:, :width])
    cot_came = came[4 * depth :]
    cotan[...] = jnp.where(same, cot_keep, cot_came)
    packed[2 * depth :] = jnp.where(same, cot_came, cot_keep)


def gather_late(matchings, fourth, fifth, came, late):
    depth = fourth.shape[-2]
    late[0] = fourth[...]
    for row in range(2):
        at = choice(matchings, 5, row)
        for slot, both in enumerate((at, 1 - at)):
            if row == 0:
                late[1, slot, row] = fifth[both]
            else:
                late[1, slot, row] = came[pl.ds(pl.multiple_of(both * depth, depth), depth)]


def total(parts, place, slot, row):
    parts = [parts[chip, place, slot, row].astype(jnp.float32) for chip in range(parts.shape[0])]
    while len(parts) > 1:
        parts = [a + b for a, b in zip(parts[::2], parts[1::2])]
    return parts[0]


def unorder_late(matchings, parts, rows):
    for place in range(2):
        for row in range(2):
            at = choice(matchings, 4 + place, row)
            for slot, both in enumerate((at, 1 - at)):
                rows[row, place, both] = total(parts, 1 + place, slot, row).astype(rows.dtype)


def finish(matchings, parts_low, parts_high, keep, came, out):
    _, low, _ = bits()
    depth = out.shape[-2]
    for section in range(4):
        parts = parts_low if section < 3 else parts_high
        for row in range(2):
            at = choice(matchings, section, row)
            for slot, both in enumerate((at, 1 - at)):
                out[section, row ^ low, both] = total(parts, section % 3, slot, row)
    for place in range(2):
        for both in range(2):
            out[4 + place, low, both] = keep[place, both].astype(jnp.float32)
            given = came[pl.ds((2 * place + both) * depth, depth)]
            out[4 + place, 1 - low, both] = given.astype(jnp.float32)


def local(kernel, matchings, *arrays, outs):
    whole = pl.BlockSpec(memory_space=pltpu.VMEM)
    scalars = () if matchings is None else (matchings,)
    moved = sum(math.prod(x.shape) * x.dtype.itemsize for x in (*arrays, *outs))
    result = pl.pallas_call(
        kernel,
        out_shape=outs,
        in_specs=[pl.BlockSpec(memory_space=pltpu.SMEM)] * len(scalars) + [whole] * len(arrays),
        out_specs=[whole] * len(outs),
        cost_estimate=pl.CostEstimate(flops=0, bytes_accessed=moved, transcendentals=0),
        compiler_params=pltpu.CompilerParams(vmem_limit_bytes=16 * 2**20),
    )(*scalars, *arrays)
    return result[0] if len(outs) == 1 else result


def core_half(terms, core):
    count, both, per_dev, size, depth, width = terms.shape
    parts = terms.reshape(count, both, per_dev, size // 2, 2, depth, width)
    half = jnp.where(core == 1, parts[:, :, :, :, 1], parts[:, :, :, :, 0])
    return jnp.moveaxis(half, 3, 0)


def chip_sum(terms):
    count, both, per_dev, depth, width = terms.shape
    size = lax.axis_size("tok")
    core = lax.axis_index("tok") & 1
    terms = terms.reshape(count, both, per_dev, size, depth // size, width)
    came = lax.ppermute(core_half(terms, 1 - core), "tok", [(source, source ^ 1) for source in range(size)])
    return (core_half(terms, core).astype(jnp.float32) + came.astype(jnp.float32)).astype(jnp.bfloat16)


def all_parts(chip):
    size = lax.axis_size("tok")
    groups = [list(range(c, size, 2)) for c in range(2)]
    return lax.all_to_all(chip, "tok", 0, 0, axis_index_groups=groups)


def body(activations, weights, matchings, cotangent):
    depth, width = weights.shape[3:]
    tokens = activations.shape[0]
    bf16 = jnp.bfloat16
    _, low, high = bits()
    low, same = low == 1, low == high

    def shape(*dims, dtype=bf16):
        return jax.ShapeDtypeStruct((*dims, width), dtype)

    first, rest, keep, send = local(
        order_early,
        matchings,
        weights,
        outs=[shape(1, 2, 2, depth), shape(3, 2, 2, depth), shape(2, 2, depth), shape(4 * depth)],
    )
    packed = local(pack_late, None, send, cotangent, outs=[shape(4 * depth + tokens)])
    came = flip(packed, 3)
    full = list(lax.all_gather(first, "tok", axis=3, tiled=True))
    full += list(lax.all_gather(rest, "tok", axis=3, tiled=True))

    left, right = activations[:, :width], activations[:, width:]
    value = jnp.stack([jnp.where(low, right, left), jnp.where(low, left, right)])
    other = value[::-1]
    inputs = [(value, other)]
    value = (dot(value, full[0][0]) + dot(other, full[0][1])).astype(bf16)

    fourth, fifth, packed, cotan0 = local(
        between,
        matchings,
        keep,
        came,
        cotangent,
        outs=[shape(2, 2, depth), shape(2, depth), shape(2 * depth + tokens), shape(tokens)],
    )
    came = flip(packed, 4)
    cotan1 = came[2 * depth :]
    late = local(gather_late, matchings, fourth, fifth, came, outs=[shape(2, 2, 2, depth)])
    full += list(lax.all_gather(late, "tok", axis=3, tiled=True))

    for section in range(1, 4):
        other = flip(value, section - 1)
        inputs.append((value, other))
        full[section] = after(full[section], value)
        own_w, other_w = full[section][0], full[section][1]
        if section < 3:
            value = (dot(value, own_w) + dot(other, other_w)).astype(bf16)
        else:
            send = (dot(value[1], own_w[1]) + dot(other[1], other_w[1])).astype(bf16)
            keep = (dot(value[0], own_w[0]) + dot(other[0], other_w[0])).astype(bf16)
    came = flip(send, 3)
    inputs.append((keep, came))
    send_w = after(full[4][:, 1], send)
    send = (dot(keep, send_w[0]) + dot(came, send_w[1])).astype(bf16)
    keep_w = after(full[4][:, 0], send)
    keep = (dot(keep, keep_w[0]) + dot(came, keep_w[1])).astype(bf16)
    full[4] = [[keep_w[slot], send_w[slot]] for slot in range(2)]
    came = flip(send, 4)
    inputs.append((keep, came))
    full[5] = after(full[5], send)
    own_w, other_w = full[5][0], full[5][1]

    results, grads = [], []
    for row, cotan in enumerate((cotan0, cotan1)):
        final = dot(keep, own_w[row]) + dot(came, other_w[row])
        results.append(jax.nn.gelu(final).astype(bf16))
        back_fn = jax.vjp(jax.nn.gelu, final)[1]
        grads.append(back_fn(cotan.astype(jnp.float32))[0].astype(bf16))

    terms = [None] * SECTIONS
    for section in (5, 4):
        own_w, other_w = full[section][0], full[section][1]
        sent = (dot_back(grads[0], other_w[0]) + dot_back(grads[1], other_w[1])).astype(bf16)
        back = flip(sent, section - 1)
        if section == 5:
            grads = [after(grad, sent) for grad in grads]
        kept = (dot_back(grads[0], own_w[0]) + dot_back(grads[1], own_w[1])).astype(bf16)
        terms[section] = jnp.stack(
            [jnp.stack([dot_rows(part, grad) for grad in grads]) for part in inputs[section]]
        )
        grads = [kept, back]
    grad = jnp.stack(grads)
    for section in (3, 2, 1):
        own_w, other_w = full[section][0], full[section][1]
        sent = dot_back(grad, other_w).astype(bf16)
        back = flip(sent, section - 1)
        terms[section] = jnp.stack([dot_rows(part, grad) for part in inputs[section]])
        if section == 3:
            chip = chip_sum(jnp.stack(terms[3:]))
            parts_high = all_parts(chip)
        grad = (dot_back(grad, own_w) + back.astype(jnp.float32)).astype(bf16)
        if section == 2:
            grad = after(grad, chip)
    terms[0] = jnp.stack([dot_rows(part, grad) for part in inputs[0]])
    chip = after(chip_sum(jnp.stack(terms[:3])), parts_high)
    parts_low = all_parts(chip)

    out_came = flip(results[1], 4)
    out_keep, out_send = jnp.where(same, results[0], out_came), jnp.where(same, out_came, results[0])
    out_came = flip(after(out_send, chip), 3)
    result = jnp.concatenate([jnp.where(low, out_came, out_keep), jnp.where(low, out_keep, out_came)], axis=1)

    rows = local(unorder_late, matchings, parts_high, outs=[shape(2, 2, 2, depth)])
    row0, row1 = rows[0], jnp.stack([rows[1, 0], flip(rows[1, 1], 4)])
    keep, send = jnp.where(same, row0, row1), jnp.where(same, row1, row0)
    came = flip(send, 3).reshape(4 * depth, width)
    weight_grad = local(
        finish, matchings, parts_low, parts_high, keep, came, outs=[shape(6, 2, 2, depth, dtype=jnp.float32)]
    )

    grad = after(grad, chip)
    own_w, other_w = full[0][0], full[0][1]
    first, second = [
        (dot_back(grad[r], own_w[r]) + dot_back(grad[1 - r], other_w[1 - r])).astype(bf16) for r in range(2)
    ]
    input_grad = jnp.concatenate([jnp.where(low, second, first), jnp.where(low, first, second)], axis=1)
    return result, input_grad, weight_grad


def solution(mesh):
    placed = (P("tok", "blk"), P(None, "blk", None, "tok", None), P(), P("tok", "blk"))
    return jax.shard_map(
        body,
        mesh=mesh,
        in_specs=placed,
        out_specs=(P("tok", "blk"), P("tok", "blk"), P(None, "blk", None, "tok", None)),
        check_vma=False,
    )
```
